512 devices in a mesh: member: 4 (over y_lo), space: 128 (over z, y_hi, x, core).
Axes of the slice: x: 4, y: 8 (y_hi: 2, y_lo: 4; y = y_hi * 4 + y_lo), z: 8, core: 2. Of those that a mesh axis runs over, the one named last changes fastest.
Arguments:
- ensemble_prediction: bfloat16 [4, 300, 2048, 128], P('member', None, 'space'), may hold values from -6 to 6
- observed_analysis: bfloat16 [300, 2048, 128], P(None, 'space'), may hold values from -6 to 6
- validity_flags: int32 [2, 2048, 128], P(None, 'space'), may hold values from 0 to 1, as said below
Outputs:
- point_score: float32 [300, 2048, 128], P(None, 'space')
- channel_loss: float32 [300], replicated
The draws below stay inside these ranges and needn't reach their ends.
Inputs may be any that keep to these rules, and one draw needn't show every extreme that they name: `validity_flags`: 0 or 1 for each point and group; every point of latitude row 180 is valid in both groups.
All inputs are finite; a program needn't handle non-finite values.
Results may differ from the reference program's by a relative error of at most 0.0003.
Values may be sent and summed in bfloat16 or wider, within the bound.
No kernel may reach another device: no remote copies, remote signals or barrier semaphores. Data moves between devices by JAX's collectives and lax.ppermute only.
A program may use at most 64 MiB of HBM per device.

```python
import jax
import jax.numpy as jnp

VARIABLE_NUMBER = 300
ATMOS = 180
GROUPS = 2
TILE_SITES = 128
LON = 720
TILE_NUMBER = 2048
LAT = 360
ENSEMBLE_SIZE = 4


def draw_validity_flags(key, part):
    position = jnp.arange(TILE_NUMBER * TILE_SITES, dtype=jnp.int32).reshape(TILE_NUMBER, TILE_SITES)
    lat_row = position // LON
    atmos_thr = 300 + 650 * lat_row // LAT
    ocean_thr = 150 + 750 * lat_row // LAT
    thresholds = jnp.stack([atmos_thr, ocean_thr])
    rolled = jax.random.randint(jax.random.fold_in(key, 17), (GROUPS, TILE_NUMBER, TILE_SITES), 0, 1000)
    drawn = (rolled < thresholds).astype(jnp.int32)
    middle = (lat_row == LAT // 2)[None]
    return jnp.where(middle, 1, drawn).astype(jnp.int32)


def level_of(rng, dims, shards, least, top_value):
    def one(dim, parts):
        steps = jax.random.uniform(jax.random.fold_in(jax.random.fold_in(rng, 6), dim), (parts,), jnp.float32, least / len(shards), top_value / len(shards))
        return jnp.repeat(jnp.exp(steps), dims[dim] // parts).reshape((-1,) + (1,) * (len(dims) - dim - 1))

    level = one(*shards[0])
    for cut in shards[1:]:
        level = level * one(*cut)
    return level


def noise(stream_key, extent, deviation, bound, split=(), held_as=jnp.bfloat16):
    values = deviation * jax.random.normal(stream_key, extent, jnp.float32)
    if split:
        values = values * level_of(stream_key, extent, split, -0.22, 0.18)
    return jnp.clip(values, -bound, bound).astype(held_as)


def setup_inputs(seed: int = 0) -> dict:
    key_of = jax.random.split(jax.random.key(seed), 4)
    return {
        "ensemble_prediction": noise(key_of[0], (ENSEMBLE_SIZE, VARIABLE_NUMBER, TILE_NUMBER, TILE_SITES), 1.0, 6.0, ((0, 4), (2, 128))),
        "observed_analysis": noise(key_of[1], (VARIABLE_NUMBER, TILE_NUMBER, TILE_SITES), 1.0, 6.0, ((1, 128),)),
        "validity_flags": draw_validity_flags(jax.random.fold_in(key_of[3], 71), 0),
    }


def reference(ensemble_prediction, observed_analysis, validity_flags):
    realization_entries = ensemble_prediction.shape[0]
    position = jnp.arange(TILE_NUMBER * TILE_SITES, dtype=jnp.int32).reshape(TILE_NUMBER, TILE_SITES)
    inside = (position < LAT * LON).astype(jnp.float32)
    lat_row = (position // LON).astype(jnp.float32)
    cosine = jnp.cos(jnp.pi * ((lat_row + 0.5) / LAT - 0.5))
    valid = inside[None] * (validity_flags > 0).astype(jnp.float32)
    weight = cosine[None] * valid
    area_sum = jnp.sum(weight, axis=(1, 2))
    count = jnp.sum(valid, axis=(1, 2))
    is_ocean = jnp.arange(VARIABLE_NUMBER, dtype=jnp.int32) >= ATMOS
    weight_chan = jnp.where(is_ocean[:, None, None], weight[1][None], weight[0][None])
    observed_real_entries = observed_analysis.astype(jnp.float32)
    accuracy_component = jnp.zeros(observed_analysis.shape, jnp.float32)
    for leading_realization in range(realization_entries):
        accuracy_component = accuracy_component + jnp.abs(ensemble_prediction[leading_realization].astype(jnp.float32) - observed_real_entries)
    dispersion_component = jnp.zeros(observed_analysis.shape, jnp.float32)
    for leading_realization in range(realization_entries):
        for trailing_realization in range(leading_realization + 1, realization_entries):
            dispersion_component = dispersion_component + jnp.abs(ensemble_prediction[leading_realization].astype(jnp.float32) - ensemble_prediction[trailing_realization].astype(jnp.float32))
    dispersion_component = 2.0 * dispersion_component
    coeff = (1.0 - 0.05 / realization_entries) / (2.0 * realization_entries * (realization_entries - 1))
    crps = accuracy_component / realization_entries - coeff * dispersion_component
    scale_chan = jnp.where(is_ocean, count[1] / area_sum[1], count[0] / area_sum[0])
    count_chan = jnp.where(is_ocean, count[1], count[0])
    point_score = crps * weight_chan * scale_chan[:, None, None]
    channel_loss = jnp.sum(point_score, axis=(1, 2)) / count_chan
    return point_score, channel_loss
```

```python
import functools

import jax
import jax.numpy as jnp
from jax import lax
from jax.experimental import pallas as pl
from jax.experimental.pallas import tpu as pltpu
from jax.sharding import Mesh
from jax.sharding import PartitionSpec as P

VARIABLE_NUMBER = 300
ATMOS = 180
TILE_SITES = 128
LON = 720
ROWS = 360
MEMBERS = 4
HALF = VARIABLE_NUMBER // 2
PARTS = 2
STEP = HALF // PARTS
SPACE = ("space_0", "space_1", "space_2", "space_3")
EVERY = ("member", *SPACE)
COEFF = (1.0 - 0.05 / MEMBERS) / (2.0 * MEMBERS * (MEMBERS - 1))
TOP = 32767.0
LEAST_EXPONENT = -120.0

NEAR_FROM_END = [(0, 1), (3, 2)]
FAR_FROM_END = [(0, 2), (3, 1)]
ACROSS = [(1, 2), (2, 1)]
TO_END = [(1, 0), (2, 3)]


def encode_kernel(first_ref, own, near_end, far_end, across, obs, weight, codes, sums, values):
    first = first_ref[0]

    def score(i, top):
        target = obs[i].astype(jnp.float32)
        a = own[i].astype(jnp.float32)
        b = near_end[i].astype(jnp.float32)
        c = far_end[i].astype(jnp.float32)
        d = across[i].astype(jnp.float32)
        skill = jnp.abs(a - target) + jnp.abs(b - target) + jnp.abs(c - target) + jnp.abs(d - target)
        low_ab, high_ab = jnp.minimum(a, b), jnp.maximum(a, b)
        low_cd, high_cd = jnp.minimum(c, d), jnp.maximum(c, d)
        outer = jnp.maximum(high_ab, high_cd) - jnp.minimum(low_ab, low_cd)
        inner = jnp.abs(jnp.minimum(high_ab, high_cd) - jnp.maximum(low_ab, low_cd))
        group = (first + i >= ATMOS).astype(jnp.int32)
        value = (skill * (1.0 / MEMBERS) - (2.0 * COEFF) * (3.0 * outer + inner)) * weight[group]
        values[i] = value
        sums[pl.ds(i, 1), :] = jnp.sum(value, axis=0, keepdims=True)
        return jnp.maximum(top, jnp.abs(value))

    top = lax.fori_loop(0, STEP, score, jnp.zeros(values.shape[1:], jnp.float32), unroll=5)
    top = jnp.broadcast_to(jnp.max(top, keepdims=True), top.shape)
    k = jnp.where(top > 0.0, jnp.ceil(jnp.log2(jnp.where(top > 0.0, top, 1.0))), 0.0)
    k = jnp.maximum(k, LEAST_EXPONENT)
    shrink = jnp.exp2(-k)
    codes[STEP] = k.astype(jnp.int32).astype(codes.dtype)

    def code(i, carry):
        value = values[i]
        root = jnp.sqrt(jnp.sqrt(jnp.abs(value) * shrink))
        steps = jnp.minimum(root * TOP + 0.5, TOP)
        steps = jnp.where(value < 0.0, -steps, steps)
        codes[i] = steps.astype(jnp.int32).astype(codes.dtype)
        return carry

    lax.fori_loop(0, STEP, code, 0, unroll=5)


def encode(first, own, near_end, far_end, across, obs, weight):
    vmem = pl.BlockSpec(memory_space=pltpu.VMEM)
    return pl.pallas_call(
        encode_kernel,
        out_shape=(
            jax.ShapeDtypeStruct((STEP + 1, *obs.shape[1:]), jnp.int16),
            jax.ShapeDtypeStruct((STEP, obs.shape[2]), jnp.float32),
        ),
        in_specs=[pl.BlockSpec(memory_space=pltpu.SMEM)] + [vmem] * 6,
        out_specs=(vmem, vmem),
        scratch_shapes=[pltpu.VMEM(obs.shape, jnp.float32)],
        compiler_params=pltpu.CompilerParams(vmem_limit_bytes=16 << 20),
        cost_estimate=pl.CostEstimate(flops=30 * obs.size, bytes_accessed=14 * obs.size, transcendentals=2 * obs.size),
    )(first, own, near_end, far_end, across, obs, weight)


def decode_kernel(where_ref, scale, mine, sent, out_before, out):
    del out_before
    first = where_ref[0] * STEP

    def channels(codes):
        unit = jnp.exp2(codes[STEP].astype(jnp.float32)) * (1.0 / TOP**4)
        units = (unit * scale[0], unit * scale[1])

        def channel(i, carry):
            steps = codes[i].astype(jnp.float32)
            square = steps * steps
            ocean = first + i >= ATMOS
            out[i] = (steps * jnp.abs(steps)) * square * jnp.where(ocean, units[1], units[0])
            return carry

        lax.fori_loop(0, STEP, channel, 0, unroll=5)

    @pl.when(where_ref[1] == 1)
    def _():
        channels(mine)

    @pl.when(where_ref[1] == 0)
    def _():
        channels(sent)


def decode(where, scale, mine, sent, out):
    rows, sites = mine.shape[1:]
    vmem = pl.BlockSpec(memory_space=pltpu.VMEM)
    shape = jax.ShapeDtypeStruct((VARIABLE_NUMBER, rows, sites), jnp.float32)
    first = out is None
    codes_spec = pl.BlockSpec(mine.shape, lambda g, w: (0, 0, 0))
    kernel = decode_kernel
    if first:
        def kernel(where_ref, scale, mine, sent, out):
            decode_kernel(where_ref, scale, mine, sent, None, out)
    return pl.pallas_call(
        kernel,
        out_shape=shape,
        grid_spec=pltpu.PrefetchScalarGridSpec(
            num_scalar_prefetch=1,
            grid=(1,),
            in_specs=[pl.BlockSpec(memory_space=pltpu.SMEM), codes_spec, codes_spec]
            + ([] if first else [pl.BlockSpec(memory_space=pl.ANY)]),
            out_specs=pl.BlockSpec((STEP, rows, sites), lambda g, w: (w[0], 0, 0)),
        ),
        input_output_aliases={} if first else {4: 0},
        compiler_params=pltpu.CompilerParams(vmem_limit_bytes=16 << 20),
        cost_estimate=pl.CostEstimate(flops=8 * mine.size, bytes_accessed=8 * mine.size, transcendentals=0),
    )(where, scale, mine, sent, *(() if first else (out,)))


def per_channel(values):
    is_ocean = jnp.arange(VARIABLE_NUMBER, dtype=jnp.int32) >= ATMOS
    return jnp.where(is_ocean, values[1], values[0])


def shards(ensemble_prediction, observed_analysis, validity_flags):
    blocks_here = observed_analysis.shape[1]
    member = lax.axis_index("member")
    side = member // 2
    middle = ((member == 1) | (member == 2)).astype(jnp.int32)
    prediction = ensemble_prediction[0]

    def cut(array, half, part):
        return lax.dynamic_slice_in_dim(array, half * HALF + part * STEP, STEP, 0)

    arrived = []
    for part in range(PARTS):
        near, far = cut(prediction, side, part), cut(prediction, 1 - side, part)
        across = lax.ppermute(far, "member", ACROSS)
        far_end = lax.ppermute(far, "member", FAR_FROM_END)
        near_end = lax.ppermute(near, "member", NEAR_FROM_END)
        arrived.append((near, near_end, far_end, across))

    first_point = lax.axis_index(SPACE) * (blocks_here * TILE_SITES)
    position = first_point + jnp.arange(blocks_here * TILE_SITES, dtype=jnp.int32).reshape(
        blocks_here, TILE_SITES
    )
    inside = (position < ROWS * LON).astype(jnp.float32)
    lat_row = (position // LON).astype(jnp.float32)
    cosine = jnp.cos(jnp.pi * ((lat_row + 0.5) / ROWS - 0.5))
    valid = inside[None] * (validity_flags > 0).astype(jnp.float32)
    weight = cosine[None] * valid
    totals = lax.psum(jnp.concatenate([jnp.sum(weight, axis=(1, 2)), jnp.sum(valid, axis=(1, 2))]), SPACE)
    area_sum, count = totals[:2], totals[2:]
    scale = count / area_sum

    out = None
    sums = []
    codes_here = []
    for part in range(PARTS):
        first = side * HALF + part * STEP
        codes, rows = encode(first[None], *arrived[part], cut(observed_analysis, side, part), weight)
        codes_here.append(codes)
        sums.append(rows)
    moved = []
    for part in range(PARTS):
        codes = codes_here[part]
        over = lax.ppermute(codes, "member", ACROSS)
        near_sent = lax.ppermute(codes, "member", TO_END)
        far_sent = lax.ppermute(over, "member", TO_END)
        moved.append((codes, near_sent, over, far_sent))
    for part in range(PARTS):
        codes, near_sent, over, far_sent = moved[part]
        out = decode(jnp.stack([side * PARTS + part, middle]), scale, codes, near_sent, out)
    for part in range(PARTS):
        codes, near_sent, over, far_sent = moved[part]
        out = decode(jnp.stack([(1 - side) * PARTS + part, middle]), scale, over, far_sent, out)

    here = jnp.sum(jnp.concatenate(sums), axis=1)
    here = jnp.where(middle == 1, here, 0.0)
    spread_out = lax.dynamic_update_slice_in_dim(jnp.zeros((VARIABLE_NUMBER,), jnp.float32), here, side * HALF, 0)
    channel_loss = lax.psum(spread_out, EVERY) / per_channel(area_sum)
    return (out, channel_loss)


def solution(mesh):
    split = Mesh(
        mesh.devices.reshape(mesh.shape["member"], 8, 2, 4, 2),
        ("member", "space_0", "space_1", "space_2", "space_3"),
    )
    return jax.shard_map(
        shards,
        mesh=split,
        in_specs=(P("member", None, SPACE, None), P(None, SPACE, None), P(None, SPACE, None)),
        out_specs=(P(None, SPACE, None), P()),
        check_vma=False,
    )
```

```python
import jax
import jax.numpy as jnp
from jax import lax
from jax.experimental import pallas as pl
from jax.experimental.pallas import tpu as pltpu
from jax.sharding import Mesh
from jax.sharding import PartitionSpec as P

VARIABLE_NUMBER = 300
ATMOS = 180
TILE_SITES = 128
LON = 720
ROWS = 360
MEMBERS = 4
SHARE = VARIABLE_NUMBER // MEMBERS
SPACE = ("space_0", "space_1", "space_2", "space_3")
ALONG_ZX = ("space_0", "space_2", "space_3")
ALONG_Y = ("member", "space_1")
COEFF = (1.0 - 0.05 / MEMBERS) / (2.0 * MEMBERS * (MEMBERS - 1))
TOP = 32767.0
LEAST_EXPONENT = -120.0


def encode_kernel(member, forecasts, obs, weight, codes, partial, values, rows):
    first = member[0] * SHARE

    def score(i, top):
        target = obs[i].astype(jnp.float32)
        a, b, c, d = (forecasts[m, i].astype(jnp.float32) for m in range(MEMBERS))
        skill = jnp.abs(a - target) + jnp.abs(b - target) + jnp.abs(c - target) + jnp.abs(d - target)
        low_ab, high_ab = jnp.minimum(a, b), jnp.maximum(a, b)
        low_cd, high_cd = jnp.minimum(c, d), jnp.maximum(c, d)
        outer = jnp.maximum(high_ab, high_cd) - jnp.minimum(low_ab, low_cd)
        inner = jnp.abs(jnp.minimum(high_ab, high_cd) - jnp.maximum(low_ab, low_cd))
        group = (first + i >= ATMOS).astype(jnp.int32)
        value = (skill * (1.0 / MEMBERS) - (2.0 * COEFF) * (3.0 * outer + inner)) * weight[group]
        values[i] = value
        rows[pl.ds(i, 1), :] = jnp.sum(value, axis=0, keepdims=True)
        return jnp.maximum(top, jnp.abs(value))

    rows[...] = jnp.zeros(rows.shape, jnp.float32)
    top = lax.fori_loop(0, SHARE, score, jnp.zeros(values.shape[1:], jnp.float32), unroll=5)
    for g in range(2):
        rows[SHARE + g : SHARE + g + 1, :] = jnp.sum(weight[g], axis=0, keepdims=True)
        valid = (weight[g] > 0.0).astype(jnp.float32)
        rows[SHARE + 2 + g : SHARE + 3 + g, :] = jnp.sum(valid, axis=0, keepdims=True)
    ones = jnp.ones((8, TILE_SITES), jnp.float32)
    partial[...] = lax.dot_general(
        ones, rows[...], (((1,), (1,)), ((), ())), precision=lax.Precision.HIGHEST, preferred_element_type=jnp.float32
    )

    top = jnp.broadcast_to(jnp.max(top, keepdims=True), top.shape)
    k = jnp.where(top > 0.0, jnp.ceil(jnp.log2(jnp.where(top > 0.0, top, 1.0))), 0.0)
    k = jnp.maximum(k, LEAST_EXPONENT)
    shrink = jnp.exp2(-k)
    exponent = k.astype(jnp.int32).astype(codes.dtype)
    for m in range(MEMBERS):
        codes[m, SHARE] = exponent

    def code(i, carry):
        value = values[i]
        root = jnp.sqrt(jnp.sqrt(jnp.abs(value) * shrink))
        steps = jnp.minimum(root * TOP + 0.5, TOP)
        steps = jnp.where(value < 0.0, -steps, steps).astype(jnp.int32).astype(codes.dtype)
        for m in range(MEMBERS):
            codes[m, i] = steps
        return carry

    lax.fori_loop(0, SHARE, code, 0, unroll=5)


def encode(member, forecasts, obs, weight):
    blocks, sites = obs.shape[1:]
    share = (SHARE, blocks, sites)
    return pl.pallas_call(
        encode_kernel,
        out_shape=(
            jax.ShapeDtypeStruct((MEMBERS, SHARE + 1, blocks, sites), jnp.int16),
            jax.ShapeDtypeStruct((8, sites), jnp.float32),
        ),
        grid_spec=pltpu.PrefetchScalarGridSpec(
            num_scalar_prefetch=1,
            grid=(1,),
            in_specs=[
                pl.BlockSpec((MEMBERS, *share), lambda g, m: (0, 0, 0, 0)),
                pl.BlockSpec(share, lambda g, m: (m[0], 0, 0)),
                pl.BlockSpec(weight.shape, lambda g, m: (0, 0, 0)),
            ],
            out_specs=(
                pl.BlockSpec((MEMBERS, SHARE + 1, blocks, sites), lambda g, m: (0, 0, 0, 0)),
                pl.BlockSpec((8, sites), lambda g, m: (0, 0)),
            ),
            scratch_shapes=[pltpu.VMEM(share, jnp.float32), pltpu.VMEM((sites, sites), jnp.float32)],
        ),
        compiler_params=pltpu.CompilerParams(vmem_limit_bytes=24 << 20),
        cost_estimate=pl.CostEstimate(
            flops=30 * SHARE * blocks * sites, bytes_accessed=14 * SHARE * blocks * sites, transcendentals=0
        ),
    )(member, forecasts, obs, weight)


def decode_kernel(scale, codes, out):
    first = pl.program_id(0) * SHARE
    unit = jnp.exp2(codes[0, SHARE].astype(jnp.float32)) * (1.0 / TOP**4)

    def channel(i, carry):
        steps = codes[0, i].astype(jnp.float32)
        square = steps * steps
        group = (first + i >= ATMOS).astype(jnp.int32)
        out[i] = (steps * jnp.abs(steps)) * square * (unit * scale[group])
        return carry

    lax.fori_loop(0, SHARE, channel, 0, unroll=5)


def decode(scale, codes):
    blocks, sites = codes.shape[2:]
    return pl.pallas_call(
        decode_kernel,
        out_shape=jax.ShapeDtypeStruct((VARIABLE_NUMBER, blocks, sites), jnp.float32),
        grid=(MEMBERS,),
        in_specs=[
            pl.BlockSpec(memory_space=pltpu.SMEM),
            pl.BlockSpec((1, SHARE + 1, blocks, sites), lambda m: (m, 0, 0, 0)),
        ],
        out_specs=pl.BlockSpec((SHARE, blocks, sites), lambda m: (m, 0, 0)),
        compiler_params=pltpu.CompilerParams(vmem_limit_bytes=24 << 20),
        cost_estimate=pl.CostEstimate(
            flops=8 * codes.size, bytes_accessed=6 * codes.size, transcendentals=0
        ),
    )(scale, codes)


def from_each(row, axes):
    copies = jnp.broadcast_to(row[None], (lax.axis_size(axes), *row.shape))
    return lax.all_to_all(copies, axes, split_axis=0, concat_axis=0, tiled=True)


def shards(ensemble_prediction, observed_analysis, validity_flags):
    blocks_here = observed_analysis.shape[1]
    forecasts = lax.all_to_all(ensemble_prediction[0], "member", split_axis=0, concat_axis=0, tiled=True)
    forecasts = forecasts.reshape(MEMBERS, SHARE, *forecasts.shape[1:])

    first_point = lax.axis_index(SPACE) * (blocks_here * TILE_SITES)
    position = first_point + jnp.arange(blocks_here * TILE_SITES, dtype=jnp.int32).reshape(
        blocks_here, TILE_SITES
    )
    inside = (position < ROWS * LON).astype(jnp.float32)
    lat_row = (position // LON).astype(jnp.float32)
    cosine = jnp.cos(jnp.pi * ((lat_row + 0.5) / ROWS - 0.5))
    weight = (cosine * inside)[None] * (validity_flags > 0).astype(jnp.float32)

    member = lax.axis_index("member")[None]
    codes, partial = encode(member, forecasts, observed_analysis, weight)
    gathered = lax.all_to_all(codes, "member", split_axis=0, concat_axis=0, tiled=True)

    over_zx = jnp.sum(from_each(partial[:1], ALONG_ZX), axis=0)
    over_y = from_each(over_zx, ALONG_Y).reshape(MEMBERS, -1, TILE_SITES)
    totals = jnp.sum(over_y, axis=1)
    area_sum = totals[0, SHARE : SHARE + 2]
    count = totals[0, SHARE + 2 : SHARE + 4]
    point_score = decode(count / area_sum, gathered)
    by_member = jnp.arange(VARIABLE_NUMBER, dtype=jnp.int32) >= ATMOS
    channel_loss = totals[:, :SHARE].reshape(VARIABLE_NUMBER) / jnp.where(by_member, area_sum[1], area_sum[0])
    return (point_score, channel_loss)


def solution(mesh):
    split = Mesh(
        mesh.devices.reshape(mesh.shape["member"], 8, 2, 4, 2),
        ("member", "space_0", "space_1", "space_2", "space_3"),
    )
    return jax.shard_map(
        shards,
        mesh=split,
        in_specs=(P("member", None, SPACE, None), P(None, SPACE, None), P(None, SPACE, None)),
        out_specs=(P(None, SPACE, None), P()),
        check_vma=False,
    )
```

```python
import jax
import jax.numpy as jnp
from jax import lax
from jax.experimental import pallas as pl
from jax.experimental.pallas import tpu as pltpu
from jax.sharding import Mesh
from jax.sharding import PartitionSpec as P

VARIABLE_NUMBER = 300
ATMOS = 180
TILE_SITES = 128
LON = 720
ROWS = 360
MEMBERS = 4
SHARE = VARIABLE_NUMBER // MEMBERS
SPACE = ("space_0", "space_1", "space_2", "space_3")
ALONG_ZX = ("space_0", "space_2", "space_3")
ALONG_Y = ("member", "space_1")
COEFF = (1.0 - 0.05 / MEMBERS) / (2.0 * MEMBERS * (MEMBERS - 1))
TOP = 32767.0
LEAST_EXPONENT = -120.0
PAIRS = (SHARE + 1) // 2


def encode_kernel(member, forecasts, obs, weight, codes, partial, values, rows):
    first = member[0] * SHARE

    def score(i, top):
        target = obs[i].astype(jnp.float32)
        a, b, c, d = (forecasts[m, i].astype(jnp.float32) for m in range(MEMBERS))
        skill = jnp.abs(a - target) + jnp.abs(b - target) + jnp.abs(c - target) + jnp.abs(d - target)
        low_ab, high_ab = jnp.minimum(a, b), jnp.maximum(a, b)
        low_cd, high_cd = jnp.minimum(c, d), jnp.maximum(c, d)
        outer = jnp.maximum(high_ab, high_cd) - jnp.minimum(low_ab, low_cd)
        inner = jnp.abs(jnp.minimum(high_ab, high_cd) - jnp.maximum(low_ab, low_cd))
        group = (first + i >= ATMOS).astype(jnp.int32)
        value = (skill * (1.0 / MEMBERS) - (2.0 * COEFF) * (3.0 * outer + inner)) * weight[group]
        values[i] = value
        rows[pl.ds(i, 1), :] = jnp.sum(value, axis=0, keepdims=True)
        return jnp.maximum(top, jnp.abs(value))

    rows[...] = jnp.zeros(rows.shape, jnp.float32)
    top = lax.fori_loop(0, SHARE, score, jnp.zeros(values.shape[1:], jnp.float32), unroll=5)
    for g in range(2):
        rows[SHARE + g : SHARE + g + 1, :] = jnp.sum(weight[g], axis=0, keepdims=True)
        valid = (weight[g] > 0.0).astype(jnp.float32)
        rows[SHARE + 2 + g : SHARE + 3 + g, :] = jnp.sum(valid, axis=0, keepdims=True)
    ones = jnp.ones((8, TILE_SITES), jnp.float32)
    partial[...] = lax.dot_general(
        ones, rows[...], (((1,), (1,)), ((), ())), precision=lax.Precision.HIGHEST, preferred_element_type=jnp.float32
    )

    top = jnp.broadcast_to(jnp.max(top, keepdims=True), top.shape)
    k = jnp.where(top > 0.0, jnp.ceil(jnp.log2(jnp.where(top > 0.0, top, 1.0))), 0.0)
    k = jnp.maximum(k, LEAST_EXPONENT)
    shrink = jnp.exp2(-k)

    def code(value):
        root = jnp.sqrt(jnp.sqrt(jnp.abs(value) * shrink))
        steps = jnp.minimum(root * TOP + 0.5, TOP)
        return jnp.where(value < 0.0, -steps, steps).astype(jnp.int32)

    def pair(i, carry):
        codes[i] = (code(values[PAIRS + i]) << 16) | (code(values[i]) & 0xFFFF)
        return carry

    lax.fori_loop(0, PAIRS - 1, pair, 0, unroll=4)
    codes[PAIRS - 1] = (k.astype(jnp.int32) << 16) | (code(values[PAIRS - 1]) & 0xFFFF)


def encode(member, forecasts, obs, weight):
    blocks, sites = obs.shape[1:]
    share = (SHARE, blocks, sites)
    return pl.pallas_call(
        encode_kernel,
        out_shape=(
            jax.ShapeDtypeStruct((PAIRS, blocks, sites), jnp.int32),
            jax.ShapeDtypeStruct((8, sites), jnp.float32),
        ),
        grid_spec=pltpu.PrefetchScalarGridSpec(
            num_scalar_prefetch=1,
            grid=(1,),
            in_specs=[
                pl.BlockSpec((MEMBERS, *share), lambda g, m: (0, 0, 0, 0)),
                pl.BlockSpec(share, lambda g, m: (m[0], 0, 0)),
                pl.BlockSpec(weight.shape, lambda g, m: (0, 0, 0)),
            ],
            out_specs=(
                pl.BlockSpec((PAIRS, blocks, sites), lambda g, m: (0, 0, 0)),
                pl.BlockSpec((8, sites), lambda g, m: (0, 0)),
            ),
            scratch_shapes=[pltpu.VMEM(share, jnp.float32), pltpu.VMEM((sites, sites), jnp.float32)],
        ),
        compiler_params=pltpu.CompilerParams(vmem_limit_bytes=24 << 20),
        cost_estimate=pl.CostEstimate(
            flops=30 * SHARE * blocks * sites, bytes_accessed=14 * SHARE * blocks * sites, transcendentals=0
        ),
    )(member, forecasts, obs, weight)


def decode_kernel(sums, codes, out, loss, scale, units):
    step = pl.program_id(0)

    @pl.when(step == 0)
    def _():
        halves = sums.shape[0] // MEMBERS
        totals = [sum(sums[m * halves + h] for h in range(halves)) for m in range(MEMBERS)]
        lane = lax.broadcasted_iota(jnp.int32, totals[0].shape, 1)

        def at(i):
            return jnp.sum(jnp.where(lane == i, totals[0], 0.0), keepdims=True)

        area = [at(SHARE + g) for g in range(2)]
        for g in range(2):
            scale[g] = jnp.broadcast_to(at(SHARE + 2 + g) / area[g], scale.shape[1:])
        width = 3 * TILE_SITES
        channel = lax.broadcasted_iota(jnp.int32, (1, width), 1)
        wide = jnp.zeros((1, width), jnp.float32)
        blank = jnp.zeros((1, width - TILE_SITES), jnp.float32)
        for m in range(MEMBERS):
            moved = pltpu.roll(jnp.concatenate([totals[m], blank], axis=1), m * SHARE, 1)
            wide = jnp.where((channel >= m * SHARE) & (channel < (m + 1) * SHARE), moved, wide)
        loss[...] = wide / jnp.where(channel >= ATMOS, area[1], area[0])

    first = step * SHARE
    unit = jnp.exp2((codes[PAIRS - 1] >> 16).astype(jnp.float32)) * (1.0 / TOP**4)
    for g in range(2):
        units[g] = unit * scale[g]

    def write(i, code):
        steps = code.astype(jnp.float32)
        square = steps * steps
        group = (first + i >= ATMOS).astype(jnp.int32)
        out[i] = (steps * jnp.abs(steps)) * square * units[group]

    def pair(i, carry):
        both = codes[i]
        write(i, (both << 16) >> 16)
        write(PAIRS + i, both >> 16)
        return carry

    lax.fori_loop(0, PAIRS - 1, pair, 0, unroll=4)
    write(PAIRS - 1, (codes[PAIRS - 1] << 16) >> 16)


def decode(sums, codes):
    blocks, sites = codes.shape[1:]
    return pl.pallas_call(
        decode_kernel,
        out_shape=(
            jax.ShapeDtypeStruct((VARIABLE_NUMBER, blocks, sites), jnp.float32),
            jax.ShapeDtypeStruct((1, 3 * sites), jnp.float32),
        ),
        grid=(MEMBERS,),
        in_specs=[
            pl.BlockSpec(sums.shape, lambda m: (0, 0, 0)),
            pl.BlockSpec((PAIRS, blocks, sites), lambda m: (m, 0, 0)),
        ],
        out_specs=(
            pl.BlockSpec((SHARE, blocks, sites), lambda m: (m, 0, 0)),
            pl.BlockSpec((1, 3 * sites), lambda m: (0, 0)),
        ),
        scratch_shapes=[pltpu.VMEM((2, blocks, sites), jnp.float32)] * 2,
        compiler_params=pltpu.CompilerParams(vmem_limit_bytes=24 << 20),
        cost_estimate=pl.CostEstimate(
            flops=16 * codes.size, bytes_accessed=12 * codes.size, transcendentals=0
        ),
    )(sums, codes)


def from_each(row, axes):
    copies = jnp.broadcast_to(row[None], (lax.axis_size(axes), *row.shape))
    return lax.all_to_all(copies, axes, split_axis=0, concat_axis=0, tiled=True)


def shards(ensemble_prediction, observed_analysis, validity_flags):
    blocks_here = observed_analysis.shape[1]
    forecasts = lax.all_to_all(ensemble_prediction[0], "member", split_axis=0, concat_axis=0, tiled=True)
    forecasts = forecasts.reshape(MEMBERS, SHARE, *forecasts.shape[1:])

    first_point = lax.axis_index(SPACE) * (blocks_here * TILE_SITES)
    position = first_point + jnp.arange(blocks_here * TILE_SITES, dtype=jnp.int32).reshape(
        blocks_here, TILE_SITES
    )
    inside = (position < ROWS * LON).astype(jnp.float32)
    lat_row = (position // LON).astype(jnp.float32)
    cosine = jnp.cos(jnp.pi * ((lat_row + 0.5) / ROWS - 0.5))
    weight = (cosine * inside)[None] * (validity_flags > 0).astype(jnp.float32)

    member = lax.axis_index("member")[None]
    codes, partial = encode(member, forecasts, observed_analysis, weight)
    gathered = lax.all_gather(codes, "member", tiled=True)
    over_zx = jnp.sum(from_each(partial[:1], ALONG_ZX), axis=0)
    point_score, loss = decode(from_each(over_zx, ALONG_Y), gathered)
    return (point_score, loss[0, :VARIABLE_NUMBER])


def solution(mesh):
    split = Mesh(
        mesh.devices.reshape(mesh.shape["member"], 8, 2, 4, 2),
        ("member", "space_0", "space_1", "space_2", "space_3"),
    )
    return jax.shard_map(
        shards,
        mesh=split,
        in_specs=(P("member", None, SPACE, None), P(None, SPACE, None), P(None, SPACE, None)),
        out_specs=(P(None, SPACE, None), P()),
        check_vma=False,
    )
```

```python
import jax
import jax.numpy as jnp
from jax import lax
from jax.experimental import pallas as pl
from jax.experimental.pallas import tpu as pltpu
from jax.sharding import Mesh
from jax.sharding import PartitionSpec as P

VARIABLE_NUMBER = 300
ATMOS = 180
TILE_SITES = 128
LON = 720
ROWS = 360
MEMBERS = 4
SHARE = VARIABLE_NUMBER // MEMBERS
SPACE = ("space_0", "space_1", "space_2", "space_3")
ALONG_ZX = ("space_0", "space_2", "space_3")
ALONG_Y = ("member", "space_1")
COEFF = (1.0 - 0.05 / MEMBERS) / (2.0 * MEMBERS * (MEMBERS - 1))
TOP = 32767.0
BESIDE = [(m, m ^ 1) for m in range(MEMBERS)]
ACROSS = [(m, m ^ 2) for m in range(MEMBERS)]
LEAST_EXPONENT = -120.0
PAIRS = (SHARE + 1) // 2


def encode_kernel(member, forecasts, obs, weight, codes, partial, values, rows):
    first = member[0] * SHARE

    def score(i, top):
        target = obs[first + i].astype(jnp.float32)
        a, b, c, d = (forecasts[m, i].astype(jnp.float32) for m in range(MEMBERS))
        skill = jnp.abs(a - target) + jnp.abs(b - target) + jnp.abs(c - target) + jnp.abs(d - target)
        low_ab, high_ab = jnp.minimum(a, b), jnp.maximum(a, b)
        low_cd, high_cd = jnp.minimum(c, d), jnp.maximum(c, d)
        outer = jnp.maximum(high_ab, high_cd) - jnp.minimum(low_ab, low_cd)
        inner = jnp.abs(jnp.minimum(high_ab, high_cd) - jnp.maximum(low_ab, low_cd))
        group = (first + i >= ATMOS).astype(jnp.int32)
        value = (skill * (1.0 / MEMBERS) - (2.0 * COEFF) * (3.0 * outer + inner)) * weight[group]
        values[i] = value
        rows[pl.ds(i, 1), :] = jnp.sum(value, axis=0, keepdims=True)
        return jnp.maximum(top, jnp.abs(value))

    rows[...] = jnp.zeros(rows.shape, jnp.float32)
    top = lax.fori_loop(0, SHARE, score, jnp.zeros(values.shape[1:], jnp.float32), unroll=5)
    for g in range(2):
        rows[SHARE + g : SHARE + g + 1, :] = jnp.sum(weight[g], axis=0, keepdims=True)
        valid = (weight[g] > 0.0).astype(jnp.float32)
        rows[SHARE + 2 + g : SHARE + 3 + g, :] = jnp.sum(valid, axis=0, keepdims=True)
    ones = jnp.ones((8, TILE_SITES), jnp.float32)
    partial[...] = lax.dot_general(
        ones, rows[...], (((1,), (1,)), ((), ())), precision=lax.Precision.HIGHEST, preferred_element_type=jnp.float32
    )

    top = jnp.broadcast_to(jnp.max(top, keepdims=True), top.shape)
    k = jnp.where(top > 0.0, jnp.ceil(jnp.log2(jnp.where(top > 0.0, top, 1.0))), 0.0)
    k = jnp.maximum(k, LEAST_EXPONENT)
    shrink = jnp.exp2(-k)

    def code(value):
        root = jnp.sqrt(jnp.sqrt(jnp.abs(value) * shrink))
        steps = jnp.minimum(root * TOP + 0.5, TOP)
        return jnp.where(value < 0.0, -steps, steps).astype(jnp.int32)

    def pair(i, carry):
        codes[i] = (code(values[PAIRS + i]) << 16) | (code(values[i]) & 0xFFFF)
        return carry

    lax.fori_loop(0, PAIRS - 1, pair, 0, unroll=4)
    codes[PAIRS - 1] = (k.astype(jnp.int32) << 16) | (code(values[PAIRS - 1]) & 0xFFFF)


def encode(member, forecasts, obs, weight):
    blocks, sites = obs.shape[1:]
    share = (SHARE, blocks, sites)
    vmem = pl.BlockSpec(memory_space=pltpu.VMEM)
    return pl.pallas_call(
        encode_kernel,
        out_shape=(
            jax.ShapeDtypeStruct((PAIRS, blocks, sites), jnp.int32),
            jax.ShapeDtypeStruct((8, sites), jnp.float32),
        ),
        in_specs=[pl.BlockSpec(memory_space=pltpu.SMEM), vmem, vmem, vmem],
        out_specs=(vmem, vmem),
        scratch_shapes=[pltpu.VMEM(share, jnp.float32), pltpu.VMEM((sites, sites), jnp.float32)],
        compiler_params=pltpu.CompilerParams(vmem_limit_bytes=24 << 20),
        cost_estimate=pl.CostEstimate(
            flops=30 * SHARE * blocks * sites, bytes_accessed=14 * SHARE * blocks * sites, transcendentals=0
        ),
    )(member, forecasts, obs, weight)


def decode_kernel(member, sums, own, beside, across, corner, out, loss, scale, units, held, copied):
    step = pl.program_id(0)
    copy = pltpu.make_async_copy(corner, held, copied)

    @pl.when(step == 0)
    def _():
        copy.start()
        halves = sums.shape[0] // MEMBERS
        totals = [sum(sums[m * halves + h] for h in range(halves)) for m in range(MEMBERS)]
        lane = lax.broadcasted_iota(jnp.int32, totals[0].shape, 1)

        def at(i):
            return jnp.sum(jnp.where(lane == i, totals[0], 0.0), keepdims=True)

        area = [at(SHARE + g) for g in range(2)]
        for g in range(2):
            scale[g] = jnp.broadcast_to(at(SHARE + 2 + g) / area[g], scale.shape[1:])
        width = 3 * TILE_SITES
        channel = lax.broadcasted_iota(jnp.int32, (1, width), 1)
        wide = jnp.zeros((1, width), jnp.float32)
        blank = jnp.zeros((1, width - TILE_SITES), jnp.float32)
        for m in range(MEMBERS):
            moved = pltpu.roll(jnp.concatenate([totals[m], blank], axis=1), m * SHARE, 1)
            wide = jnp.where((channel >= m * SHARE) & (channel < (m + 1) * SHARE), moved, wide)
        wide = wide / jnp.where(channel >= ATMOS, area[1], area[0])
        loss[...] = wide[0, :VARIABLE_NUMBER]

    first = (member[0] ^ step) * SHARE

    def share(codes):
        unit = jnp.exp2((codes[PAIRS - 1] >> 16).astype(jnp.float32)) * (1.0 / TOP**4)
        for g in range(2):
            units[g] = unit * scale[g]

        def write(i, code):
            steps = code.astype(jnp.float32)
            square = steps * steps
            group = (first + i >= ATMOS).astype(jnp.int32)
            out[i] = (steps * jnp.abs(steps)) * square * units[group]

        def pair(i, carry):
            both = codes[i]
            write(i, (both << 16) >> 16)
            write(PAIRS + i, both >> 16)
            return carry

        lax.fori_loop(0, PAIRS - 1, pair, 0, unroll=4)
        write(PAIRS - 1, (codes[PAIRS - 1] << 16) >> 16)

    for s, codes in enumerate((own, beside, across, held)):

        @pl.when(step == s)
        def _(s=s, codes=codes):
            if s == MEMBERS - 1:
                copy.wait()
            share(codes)


def decode(member, sums, shares):
    blocks, sites = shares[0].shape[1:]
    vmem = pl.BlockSpec(memory_space=pltpu.VMEM)
    return pl.pallas_call(
        decode_kernel,
        out_shape=(
            jax.ShapeDtypeStruct((VARIABLE_NUMBER, blocks, sites), jnp.float32),
            jax.ShapeDtypeStruct((VARIABLE_NUMBER,), jnp.float32),
        ),
        grid_spec=pltpu.PrefetchScalarGridSpec(
            num_scalar_prefetch=1,
            grid=(MEMBERS,),
            in_specs=[vmem] * 4 + [pl.BlockSpec(memory_space=pl.ANY)],
            out_specs=(
                pl.BlockSpec((SHARE, blocks, sites), lambda s, member: (member[0] ^ s, 0, 0)),
                pl.BlockSpec((VARIABLE_NUMBER,), lambda s, member: (0,)),
            ),
            scratch_shapes=[pltpu.VMEM((2, blocks, sites), jnp.float32)] * 2
            + [pltpu.VMEM(shares[0].shape, jnp.int32), pltpu.SemaphoreType.DMA],
        ),
        compiler_params=pltpu.CompilerParams(vmem_limit_bytes=24 << 20),
        cost_estimate=pl.CostEstimate(
            flops=64 * shares[0].size, bytes_accessed=48 * shares[0].size, transcendentals=0
        ),
    )(member, sums, *shares)


def from_each(row, axes):
    copies = jnp.broadcast_to(row[None], (lax.axis_size(axes), *row.shape))
    return lax.all_to_all(copies, axes, split_axis=0, concat_axis=0, tiled=True)


def in_one_step(always, f, *args):
    shapes = jax.eval_shape(f, *args)
    return lax.cond(always, f, lambda *args: jax.tree.map(lambda x: jnp.zeros(x.shape, x.dtype), shapes), *args)


def shards(ensemble_prediction, observed_analysis, validity_flags):
    blocks_here = observed_analysis.shape[1]
    forecasts = lax.all_to_all(ensemble_prediction[0], "member", split_axis=0, concat_axis=0, tiled=True)
    forecasts = forecasts.reshape(MEMBERS, SHARE, *forecasts.shape[1:])

    first_point = lax.axis_index(SPACE) * (blocks_here * TILE_SITES)
    position = first_point + jnp.arange(blocks_here * TILE_SITES, dtype=jnp.int32).reshape(
        blocks_here, TILE_SITES
    )
    inside = (position < ROWS * LON).astype(jnp.float32)
    lat_row = (position // LON).astype(jnp.float32)
    cosine = jnp.cos(jnp.pi * ((lat_row + 0.5) / ROWS - 0.5))
    weight = (cosine * inside)[None] * (validity_flags > 0).astype(jnp.float32)

    member = lax.axis_index("member")[None]
    codes, partial = encode(member, forecasts, observed_analysis, weight)
    always = member[0] >= 0
    across = lax.ppermute(codes, "member", ACROSS)
    beside = lax.ppermute(codes, "member", BESIDE)
    over_zx = in_one_step(always, lambda row: jnp.sum(from_each(row, ALONG_ZX), axis=0), partial[:1])

    def last_step(across, row):
        corner = lax.ppermute(across, "member", BESIDE)
        return corner, in_one_step(always, lambda row: from_each(row, ALONG_Y), row)

    corner, over_y = in_one_step(always, last_step, across, over_zx)
    point_score, loss = decode(member, over_y, (codes, beside, across, corner))
    return (point_score, loss)


def solution(mesh):
    split = Mesh(
        mesh.devices.reshape(mesh.shape["member"], 8, 2, 4, 2),
        ("member", "space_0", "space_1", "space_2", "space_3"),
    )
    return jax.shard_map(
        shards,
        mesh=split,
        in_specs=(P("member", None, SPACE, None), P(None, SPACE, None), P(None, SPACE, None)),
        out_specs=(P(None, SPACE, None), P()),
        check_vma=False,
    )
```

```python
import jax
import jax.numpy as jnp
from jax import lax
from jax.experimental import pallas as pl
from jax.experimental.pallas import tpu as pltpu
from jax.sharding import Mesh
from jax.sharding import PartitionSpec as P

VARIABLE_NUMBER = 300
ATMOS = 180
TILE_SITES = 128
LON = 720
ROWS = 360
MEMBERS = 4
SHARE = VARIABLE_NUMBER // MEMBERS
SPACE = ("space_0", "space_1", "space_2", "space_3")
ALONG_ZX = ("space_0", "space_2", "space_3")
ALONG_Y = ("member", "space_1")
COEFF = (1.0 - 0.05 / MEMBERS) / (2.0 * MEMBERS * (MEMBERS - 1))
TOP = 32767.0
BESIDE = [(m, m ^ 1) for m in range(MEMBERS)]
ACROSS = [(m, m ^ 2) for m in range(MEMBERS)]
CORNER = [(m, m ^ 3) for m in range(MEMBERS)]
REPEATS = 5
LEAST_EXPONENT = -120.0
PAIRS = (SHARE + 1) // 2


def encode_kernel(member, forecasts, obs, weight, codes, partial, values, rows):
    first = member[0] * SHARE

    def score(i, top):
        target = obs[first + i].astype(jnp.float32)
        a, b, c, d = (forecasts[m, i].astype(jnp.float32) for m in range(MEMBERS))
        skill = jnp.abs(a - target) + jnp.abs(b - target) + jnp.abs(c - target) + jnp.abs(d - target)
        low_ab, high_ab = jnp.minimum(a, b), jnp.maximum(a, b)
        low_cd, high_cd = jnp.minimum(c, d), jnp.maximum(c, d)
        outer = jnp.maximum(high_ab, high_cd) - jnp.minimum(low_ab, low_cd)
        inner = jnp.abs(jnp.minimum(high_ab, high_cd) - jnp.maximum(low_ab, low_cd))
        group = (first + i >= ATMOS).astype(jnp.int32)
        value = (skill * (1.0 / MEMBERS) - (2.0 * COEFF) * (3.0 * outer + inner)) * weight[group]
        values[i] = value
        rows[pl.ds(i, 1), :] = jnp.sum(value, axis=0, keepdims=True)
        return jnp.maximum(top, jnp.abs(value))

    rows[...] = jnp.zeros(rows.shape, jnp.float32)
    top = lax.fori_loop(0, SHARE, score, jnp.zeros(values.shape[1:], jnp.float32), unroll=5)
    for g in range(2):
        rows[SHARE + g : SHARE + g + 1, :] = jnp.sum(weight[g], axis=0, keepdims=True)
        valid = (weight[g] > 0.0).astype(jnp.float32)
        rows[SHARE + 2 + g : SHARE + 3 + g, :] = jnp.sum(valid, axis=0, keepdims=True)
    ones = jnp.ones((8, TILE_SITES), jnp.float32)
    partial[...] = lax.dot_general(
        ones, rows[...], (((1,), (1,)), ((), ())), precision=lax.Precision.HIGHEST, preferred_element_type=jnp.float32
    )

    top = jnp.broadcast_to(jnp.max(top, keepdims=True), top.shape)
    k = jnp.where(top > 0.0, jnp.ceil(jnp.log2(jnp.where(top > 0.0, top, 1.0))), 0.0)
    k = jnp.maximum(k, LEAST_EXPONENT)
    shrink = jnp.exp2(-k)

    def code(value):
        root = jnp.sqrt(jnp.sqrt(jnp.abs(value) * shrink))
        steps = jnp.minimum(root * TOP + 0.5, TOP)
        return jnp.where(value < 0.0, -steps, steps).astype(jnp.int32)

    def pair(i, carry):
        codes[i] = (code(values[PAIRS + i]) << 16) | (code(values[i]) & 0xFFFF)
        return carry

    lax.fori_loop(0, PAIRS - 1, pair, 0, unroll=4)
    codes[PAIRS - 1] = (k.astype(jnp.int32) << 16) | (code(values[PAIRS - 1]) & 0xFFFF)


def encode(member, forecasts, obs, weight):
    blocks, sites = obs.shape[1:]
    share = (SHARE, blocks, sites)
    vmem = pl.BlockSpec(memory_space=pltpu.VMEM)
    return pl.pallas_call(
        encode_kernel,
        out_shape=(
            jax.ShapeDtypeStruct((PAIRS, blocks, sites), jnp.int32),
            jax.ShapeDtypeStruct((8, sites), jnp.float32),
        ),
        in_specs=[pl.BlockSpec(memory_space=pltpu.SMEM), vmem, vmem, vmem],
        out_specs=(vmem, vmem),
        scratch_shapes=[pltpu.VMEM(share, jnp.float32), pltpu.VMEM((sites, sites), jnp.float32)],
        compiler_params=pltpu.CompilerParams(vmem_limit_bytes=24 << 20),
        cost_estimate=pl.CostEstimate(
            flops=30 * SHARE * blocks * sites, bytes_accessed=14 * SHARE * blocks * sites, transcendentals=0
        ),
    )(member, forecasts, obs, weight)


def in_order(step):
    return (step & 1) * 2 + (step >> 1)


def decode_kernel(member, sums, own, across, beside, corner, out, loss, scale, units, held, copied):
    step = pl.program_id(0)
    halves = sums.shape[0] // MEMBERS
    copies = [pltpu.make_async_copy(codes, held.at[s], copied.at[s]) for s, codes in enumerate((beside, corner))]

    def total(m):
        return sum(sums[m * halves + h] for h in range(halves))

    def at(i):
        row = total(0)
        lane = lax.broadcasted_iota(jnp.int32, row.shape, 1)
        return jnp.sum(jnp.where(lane == i, row, 0.0), keepdims=True)

    @pl.when(step == 0)
    def _():
        for copy in copies:
            copy.start()
        for g in range(2):
            scale[g] = jnp.broadcast_to(at(SHARE + 2 + g) / at(SHARE + g), scale.shape[1:])

    @pl.when(step == 1)
    def _():
        width = 3 * TILE_SITES
        channel = lax.broadcasted_iota(jnp.int32, (1, width), 1)
        wide = jnp.zeros((1, width), jnp.float32)
        blank = jnp.zeros((1, width - TILE_SITES), jnp.float32)
        for m in range(MEMBERS):
            moved = pltpu.roll(jnp.concatenate([total(m), blank], axis=1), m * SHARE, 1)
            wide = jnp.where((channel >= m * SHARE) & (channel < (m + 1) * SHARE), moved, wide)
        wide = wide / jnp.where(channel >= ATMOS, at(SHARE + 1), at(SHARE))
        loss[...] = wide[0, :VARIABLE_NUMBER]

    first = (member[0] ^ in_order(step)) * SHARE

    def share(codes):
        unit = jnp.exp2((codes[PAIRS - 1] >> 16).astype(jnp.float32)) * (1.0 / TOP**4)
        for g in range(2):
            units[g] = unit * scale[g]

        def write(i, code):
            steps = code.astype(jnp.float32)
            square = steps * steps
            group = (first + i >= ATMOS).astype(jnp.int32)
            out[i] = (steps * jnp.abs(steps)) * square * units[group]

        def pair(i, carry):
            both = codes[i]
            write(i, (both << 16) >> 16)
            write(PAIRS + i, both >> 16)
            return carry

        lax.fori_loop(0, PAIRS - 1, pair, 0, unroll=4)
        write(PAIRS - 1, (codes[PAIRS - 1] << 16) >> 16)

    for s, codes in enumerate((own, across, held.at[0], held.at[1])):

        @pl.when(step == s)
        def _(s=s, codes=codes):
            if s >= 2:
                copies[s - 2].wait()
            share(codes)


def decode(member, sums, shares):
    blocks, sites = shares[0].shape[1:]
    vmem = pl.BlockSpec(memory_space=pltpu.VMEM)
    return pl.pallas_call(
        decode_kernel,
        out_shape=(
            jax.ShapeDtypeStruct((VARIABLE_NUMBER, blocks, sites), jnp.float32),
            jax.ShapeDtypeStruct((VARIABLE_NUMBER,), jnp.float32),
        ),
        grid_spec=pltpu.PrefetchScalarGridSpec(
            num_scalar_prefetch=1,
            grid=(MEMBERS,),
            in_specs=[vmem] * 3 + [pl.BlockSpec(memory_space=pl.ANY)] * 2,
            out_specs=(
                pl.BlockSpec((SHARE, blocks, sites), lambda s, member: (member[0] ^ in_order(s), 0, 0)),
                pl.BlockSpec((VARIABLE_NUMBER,), lambda s, member: (0,)),
            ),
            scratch_shapes=[pltpu.VMEM((2, blocks, sites), jnp.float32)] * 2
            + [pltpu.VMEM((2, *shares[0].shape), jnp.int32), pltpu.SemaphoreType.DMA((2,))],
        ),
        compiler_params=pltpu.CompilerParams(vmem_limit_bytes=24 << 20),
        cost_estimate=pl.CostEstimate(
            flops=64 * shares[0].size, bytes_accessed=48 * shares[0].size, transcendentals=0
        ),
    )(member, sums, *shares)


def copied(row, number):
    return jnp.broadcast_to(row[None], (number, *row.shape))


def exchanged(copies, axes):
    return lax.all_to_all(copies, axes, split_axis=0, concat_axis=0, tiled=True)


def in_one_step(always, f, *args):
    shapes = jax.eval_shape(f, *args)
    return lax.cond(always, f, lambda *args: jax.tree.map(lambda x: jnp.zeros(x.shape, x.dtype), shapes), *args)


def shards(ensemble_prediction, observed_analysis, validity_flags):
    blocks_here = observed_analysis.shape[1]
    forecasts = lax.all_to_all(ensemble_prediction[0], "member", split_axis=0, concat_axis=0, tiled=True)
    forecasts = forecasts.reshape(MEMBERS, SHARE, *forecasts.shape[1:])

    first_point = lax.axis_index(SPACE) * (blocks_here * TILE_SITES)
    position = first_point + jnp.arange(blocks_here * TILE_SITES, dtype=jnp.int32).reshape(
        blocks_here, TILE_SITES
    )
    inside = (position < ROWS * LON).astype(jnp.float32)
    lat_row = (position // LON).astype(jnp.float32)
    cosine = jnp.cos(jnp.pi * ((lat_row + 0.5) / ROWS - 0.5))
    weight = (cosine * inside)[None] * (validity_flags > 0).astype(jnp.float32)

    member = lax.axis_index("member")[None]
    codes, partial = encode(member, forecasts, observed_analysis, weight)
    always = member[0] >= 0
    across = lax.ppermute(codes, "member", ACROSS)

    def add_up_and_send(codes, copies):
        beside = lax.ppermute(codes, "member", BESIDE)
        corner = lax.ppermute(codes, "member", CORNER)
        over_zx = jnp.sum(exchanged(copies, ALONG_ZX)[::REPEATS], axis=0)
        over_zx = copied(over_zx, lax.axis_size(ALONG_Y))
        return beside, corner, in_one_step(always, lambda copies: exchanged(copies, ALONG_Y), over_zx)

    copies = copied(partial[:1], REPEATS * lax.axis_size(ALONG_ZX))
    beside, corner, over_y = in_one_step(always, add_up_and_send, codes, copies)
    point_score, loss = decode(member, over_y, (codes, across, beside, corner))
    return (point_score, loss)


def solution(mesh):
    split = Mesh(
        mesh.devices.reshape(mesh.shape["member"], 8, 2, 4, 2),
        ("member", "space_0", "space_1", "space_2", "space_3"),
    )
    return jax.shard_map(
        shards,
        mesh=split,
        in_specs=(P("member", None, SPACE, None), P(None, SPACE, None), P(None, SPACE, None)),
        out_specs=(P(None, SPACE, None), P()),
        check_vma=False,
    )
```

```python
import jax
import jax.numpy as jnp
from jax import lax
from jax.experimental import pallas as pl
from jax.experimental.pallas import tpu as pltpu
from jax.sharding import Mesh
from jax.sharding import PartitionSpec as P

VARIABLE_NUMBER = 300
ATMOS = 180
TILE_SITES = 128
LON = 720
ROWS = 360
MEMBERS = 4
SHARE = VARIABLE_NUMBER // MEMBERS
SPACE = ("space_0", "space_1", "space_2", "space_3")
ALONG_ZX = ("space_0", "space_2")
ALONG_YC = ("member", "space_1", "space_3")
COEFF = (1.0 - 0.05 / MEMBERS) / (2.0 * MEMBERS * (MEMBERS - 1))
TOP = 32767.0
BESIDE = [(m, m ^ 1) for m in range(MEMBERS)]
ACROSS = [(m, m ^ 2) for m in range(MEMBERS)]
CORNER = [(m, m ^ 3) for m in range(MEMBERS)]
REPEATS = 10
LEAST_EXPONENT = -120.0
PAIRS = (SHARE + 1) // 2


def encode_kernel(member, forecasts, obs, weight, codes, partial, values, rows, held, copied):
    first = member[0] * SHARE

    def score(i, top):
        target = obs[first + i].astype(jnp.float32)
        a, b, c, d = (forecasts[m, i] for m in range(MEMBERS))
        low_ab, high_ab = jnp.minimum(a, b), jnp.maximum(a, b)
        low_cd, high_cd = jnp.minimum(c, d), jnp.maximum(c, d)
        least, most = jnp.minimum(low_ab, low_cd), jnp.maximum(high_ab, high_cd)
        inner = jnp.minimum(high_ab, high_cd), jnp.maximum(low_ab, low_cd)
        p, q, r, s = (x.astype(jnp.float32) for x in (least, most, *inner))
        skill = jnp.abs(p - target) + jnp.abs(q - target) + jnp.abs(r - target) + jnp.abs(s - target)
        spread = 3.0 * (q - p) + jnp.abs(r - s)
        group = (first + i >= ATMOS).astype(jnp.int32)
        value = (skill * (1.0 / MEMBERS) - (2.0 * COEFF) * spread) * weight[group]
        values[i] = value
        rows[pl.ds(i, 1), :] = jnp.sum(value, axis=0, keepdims=True)
        return jnp.maximum(top, jnp.abs(value))

    rows[...] = jnp.zeros(rows.shape, jnp.float32)
    top = lax.fori_loop(0, SHARE, score, jnp.zeros(values.shape[1:], jnp.float32), unroll=5)
    for g in range(2):
        rows[SHARE + g : SHARE + g + 1, :] = jnp.sum(weight[g], axis=0, keepdims=True)
        valid = (weight[g] > 0.0).astype(jnp.float32)
        rows[SHARE + 2 + g : SHARE + 3 + g, :] = jnp.sum(valid, axis=0, keepdims=True)
    ones = jnp.ones((8, TILE_SITES), jnp.float32)
    sums = lax.dot_general(
        ones, rows[...], (((1,), (1,)), ((), ())), precision=lax.Precision.HIGHEST, preferred_element_type=jnp.float32
    )
    held[...] = jnp.broadcast_to(sums[None, :1], held.shape)
    copy = pltpu.make_async_copy(held, partial, copied)
    copy.start()

    top = jnp.broadcast_to(jnp.max(top, keepdims=True), top.shape)
    k = jnp.where(top > 0.0, jnp.ceil(jnp.log2(jnp.where(top > 0.0, top, 1.0))), 0.0)
    k = jnp.maximum(k, LEAST_EXPONENT)
    shrink = jnp.exp2(-k)

    def code(value):
        root = jnp.sqrt(jnp.sqrt(jnp.abs(value) * shrink))
        steps = jnp.minimum(root * TOP + 0.5, TOP)
        return jnp.where(value < 0.0, -steps, steps).astype(jnp.int32)

    def pair(i, carry):
        codes[i] = (code(values[PAIRS + i]) << 16) | (code(values[i]) & 0xFFFF)
        return carry

    lax.fori_loop(0, PAIRS - 1, pair, 0, unroll=4)
    codes[PAIRS - 1] = (k.astype(jnp.int32) << 16) | (code(values[PAIRS - 1]) & 0xFFFF)
    copy.wait()


def encode(member, forecasts, obs, weight, number):
    blocks, sites = obs.shape[1:]
    share = (SHARE, blocks, sites)
    vmem = pl.BlockSpec(memory_space=pltpu.VMEM)
    return pl.pallas_call(
        encode_kernel,
        out_shape=(
            jax.ShapeDtypeStruct((PAIRS, blocks, sites), jnp.int32),
            jax.ShapeDtypeStruct((number, 1, sites), jnp.float32),
        ),
        in_specs=[pl.BlockSpec(memory_space=pltpu.SMEM), vmem, vmem, vmem],
        out_specs=(vmem, pl.BlockSpec(memory_space=pl.ANY)),
        scratch_shapes=[
            pltpu.VMEM(share, jnp.float32),
            pltpu.VMEM((sites, sites), jnp.float32),
            pltpu.VMEM((number, 1, sites), jnp.float32),
            pltpu.SemaphoreType.DMA,
        ],
        compiler_params=pltpu.CompilerParams(vmem_limit_bytes=24 << 20),
        cost_estimate=pl.CostEstimate(
            flops=30 * SHARE * blocks * sites, bytes_accessed=14 * SHARE * blocks * sites, transcendentals=0
        ),
    )(member, forecasts, obs, weight)


def in_order(step):
    return (step & 1) * 2 + (step >> 1)


def decode_kernel(member, sums, own, across, beside, corner, out, loss, scale, units, held, copied):
    step = pl.program_id(0)
    halves = sums.shape[0] // MEMBERS
    copies = [pltpu.make_async_copy(codes, held.at[s], copied.at[s]) for s, codes in enumerate((beside, corner))]

    def total(m):
        return sum(sums[m * halves + h] for h in range(halves))

    def at(i):
        row = total(0)
        lane = lax.broadcasted_iota(jnp.int32, row.shape, 1)
        return jnp.sum(jnp.where(lane == i, row, 0.0), keepdims=True)

    @pl.when(step == 0)
    def _():
        for copy in copies:
            copy.start()
        for g in range(2):
            scale[g] = jnp.broadcast_to(at(SHARE + 2 + g) / at(SHARE + g), scale.shape[1:])

    @pl.when(step == 1)
    def _():
        width = 3 * TILE_SITES
        channel = lax.broadcasted_iota(jnp.int32, (1, width), 1)
        wide = jnp.zeros((1, width), jnp.float32)
        blank = jnp.zeros((1, width - TILE_SITES), jnp.float32)
        for m in range(MEMBERS):
            moved = pltpu.roll(jnp.concatenate([total(m), blank], axis=1), m * SHARE, 1)
            wide = jnp.where((channel >= m * SHARE) & (channel < (m + 1) * SHARE), moved, wide)
        wide = wide / jnp.where(channel >= ATMOS, at(SHARE + 1), at(SHARE))
        loss[...] = wide[0, :VARIABLE_NUMBER]

    first = (member[0] ^ in_order(step)) * SHARE

    def share(codes):
        unit = jnp.exp2((codes[PAIRS - 1] >> 16).astype(jnp.float32)) * (1.0 / TOP**4)
        for g in range(2):
            units[g] = unit * scale[g]

        def write(i, code):
            steps = code.astype(jnp.float32)
            square = steps * steps
            group = (first + i >= ATMOS).astype(jnp.int32)
            out[i] = (steps * jnp.abs(steps)) * square * units[group]

        def pair(i, carry):
            both = codes[i]
            write(i, (both << 16) >> 16)
            write(PAIRS + i, both >> 16)
            return carry

        lax.fori_loop(0, PAIRS - 1, pair, 0, unroll=4)
        write(PAIRS - 1, (codes[PAIRS - 1] << 16) >> 16)

    for s, codes in enumerate((own, across, held.at[0], held.at[1])):

        @pl.when(step == s)
        def _(s=s, codes=codes):
            if s >= 2:
                copies[s - 2].wait()
            share(codes)


def decode(member, sums, shares):
    blocks, sites = shares[0].shape[1:]
    vmem = pl.BlockSpec(memory_space=pltpu.VMEM)
    return pl.pallas_call(
        decode_kernel,
        out_shape=(
            jax.ShapeDtypeStruct((VARIABLE_NUMBER, blocks, sites), jnp.float32),
            jax.ShapeDtypeStruct((VARIABLE_NUMBER,), jnp.float32),
        ),
        grid_spec=pltpu.PrefetchScalarGridSpec(
            num_scalar_prefetch=1,
            grid=(MEMBERS,),
            in_specs=[vmem] * 3 + [pl.BlockSpec(memory_space=pl.ANY)] * 2,
            out_specs=(
                pl.BlockSpec((SHARE, blocks, sites), lambda s, member: (member[0] ^ in_order(s), 0, 0)),
                pl.BlockSpec((VARIABLE_NUMBER,), lambda s, member: (0,)),
            ),
            scratch_shapes=[pltpu.VMEM((2, blocks, sites), jnp.float32)] * 2
            + [pltpu.VMEM((2, *shares[0].shape), jnp.int32), pltpu.SemaphoreType.DMA((2,))],
        ),
        compiler_params=pltpu.CompilerParams(vmem_limit_bytes=24 << 20),
        cost_estimate=pl.CostEstimate(
            flops=64 * shares[0].size, bytes_accessed=48 * shares[0].size, transcendentals=0
        ),
    )(member, sums, *shares)


def copied(row, number):
    return jnp.broadcast_to(row[None], (number, *row.shape))


def exchanged(copies, axes):
    return lax.all_to_all(copies, axes, split_axis=0, concat_axis=0, tiled=True)


def in_one_step(always, f, *args):
    shapes = jax.eval_shape(f, *args)
    return lax.cond(always, f, lambda *args: jax.tree.map(lambda x: jnp.zeros(x.shape, x.dtype), shapes), *args)


def shards(ensemble_prediction, observed_analysis, validity_flags):
    blocks_here = observed_analysis.shape[1]
    forecasts = lax.all_to_all(ensemble_prediction[0], "member", split_axis=0, concat_axis=0, tiled=True)
    forecasts = forecasts.reshape(MEMBERS, SHARE, *forecasts.shape[1:])

    first_point = lax.axis_index(SPACE) * (blocks_here * TILE_SITES)
    position = first_point + jnp.arange(blocks_here * TILE_SITES, dtype=jnp.int32).reshape(
        blocks_here, TILE_SITES
    )
    inside = (position < ROWS * LON).astype(jnp.float32)
    lat_row = (position // LON).astype(jnp.float32)
    cosine = jnp.cos(jnp.pi * ((lat_row + 0.5) / ROWS - 0.5))
    weight = (cosine * inside)[None] * (validity_flags > 0).astype(jnp.float32)

    member = lax.axis_index("member")[None]
    codes, partial = encode(
        member, forecasts, observed_analysis, weight, REPEATS * lax.axis_size(ALONG_ZX)
    )
    always = member[0] >= 0
    across = lax.ppermute(codes, "member", ACROSS)

    def add_up_and_send(codes, copies):
        beside = lax.ppermute(codes, "member", BESIDE)
        corner = lax.ppermute(codes, "member", CORNER)
        over_zx = jnp.sum(exchanged(copies, ALONG_ZX)[::REPEATS], axis=0)
        over_zx = copied(over_zx, lax.axis_size(ALONG_YC))
        return beside, corner, in_one_step(always, lambda copies: exchanged(copies, ALONG_YC), over_zx)

    beside, corner, over_yc = in_one_step(always, add_up_and_send, codes, partial)
    point_score, loss = decode(member, over_yc, (codes, across, beside, corner))
    return (point_score, loss)


def solution(mesh):
    split = Mesh(
        mesh.devices.reshape(mesh.shape["member"], 8, 2, 4, 2),
        ("member", "space_0", "space_1", "space_2", "space_3"),
    )
    return jax.shard_map(
        shards,
        mesh=split,
        in_specs=(P("member", None, SPACE, None), P(None, SPACE, None), P(None, SPACE, None)),
        out_specs=(P(None, SPACE, None), P()),
        check_vma=False,
    )
```

```python
import jax
import jax.numpy as jnp
from jax import lax
from jax.experimental import pallas as pl
from jax.experimental.pallas import tpu as pltpu
from jax.sharding import Mesh
from jax.sharding import PartitionSpec as P

VARIABLE_NUMBER = 300
ATMOS = 180
TILE_SITES = 128
LON = 720
ROWS = 360
MEMBERS = 4
SHARE = VARIABLE_NUMBER // MEMBERS
SPACE = ("space_0", "space_1", "space_2", "space_3")
ALONG_ZX = ("space_0", "space_2")
ALONG_YC = ("member", "space_1", "space_3")
COEFF = (1.0 - 0.05 / MEMBERS) / (2.0 * MEMBERS * (MEMBERS - 1))
TOP = 32767.0
BESIDE = [(m, m ^ 1) for m in range(MEMBERS)]
ACROSS = [(m, m ^ 2) for m in range(MEMBERS)]
CORNER = [(m, m ^ 3) for m in range(MEMBERS)]
REPEATS = 10
LEAST_EXPONENT = -120.0
PAIRS = (SHARE + 1) // 2


def encode_kernel(member, forecasts, obs, weight, codes, partial, values, rows, held, copied):
    first = member[0] * SHARE

    def score(i, top):
        target = obs[first + i].astype(jnp.float32)
        a, b, c, d = (forecasts[m, i] for m in range(MEMBERS))
        low_ab, high_ab = jnp.minimum(a, b), jnp.maximum(a, b)
        low_cd, high_cd = jnp.minimum(c, d), jnp.maximum(c, d)
        least, most = jnp.minimum(low_ab, low_cd), jnp.maximum(high_ab, high_cd)
        inner = jnp.minimum(high_ab, high_cd), jnp.maximum(low_ab, low_cd)
        p, q, r, s = (x.astype(jnp.float32) for x in (least, most, *inner))
        skill = jnp.abs(p - target) + jnp.abs(q - target) + jnp.abs(r - target) + jnp.abs(s - target)
        spread = 3.0 * (q - p) + jnp.abs(r - s)
        group = (first + i >= ATMOS).astype(jnp.int32)
        value = (skill * (1.0 / MEMBERS) - (2.0 * COEFF) * spread) * weight[group]
        values[i] = value
        rows[pl.ds(i, 1), :] = jnp.sum(value, axis=0, keepdims=True)
        return jnp.maximum(top, jnp.abs(value))

    rows[...] = jnp.zeros(rows.shape, jnp.float32)
    top = lax.fori_loop(0, SHARE, score, jnp.zeros(values.shape[1:], jnp.float32), unroll=5)
    for g in range(2):
        rows[SHARE + g : SHARE + g + 1, :] = jnp.sum(weight[g], axis=0, keepdims=True)
        valid = (weight[g] > 0.0).astype(jnp.float32)
        rows[SHARE + 2 + g : SHARE + 3 + g, :] = jnp.sum(valid, axis=0, keepdims=True)
    ones = jnp.ones((8, TILE_SITES), jnp.float32)
    sums = lax.dot_general(
        ones, rows[...], (((1,), (1,)), ((), ())), precision=lax.Precision.HIGHEST, preferred_element_type=jnp.float32
    )
    held[...] = jnp.broadcast_to(sums[None, :1], held.shape)
    copy = pltpu.make_async_copy(held, partial, copied)
    copy.start()

    top = jnp.broadcast_to(jnp.max(top, keepdims=True), top.shape)
    k = jnp.where(top > 0.0, jnp.ceil(jnp.log2(jnp.where(top > 0.0, top, 1.0))), 0.0)
    k = jnp.maximum(k, LEAST_EXPONENT)
    shrink = jnp.exp2(-k)

    def code(value):
        root = jnp.sqrt(jnp.sqrt(jnp.abs(value) * shrink))
        steps = jnp.minimum(root * TOP + 0.5, TOP)
        return jnp.where(value < 0.0, -steps, steps).astype(jnp.int32)

    def pair(i, carry):
        codes[i] = (code(values[PAIRS + i]) << 16) | (code(values[i]) & 0xFFFF)
        return carry

    lax.fori_loop(0, PAIRS - 1, pair, 0, unroll=4)
    codes[PAIRS - 1] = (k.astype(jnp.int32) << 16) | (code(values[PAIRS - 1]) & 0xFFFF)
    copy.wait()


def encode(member, forecasts, obs, weight, number):
    blocks, sites = obs.shape[1:]
    share = (SHARE, blocks, sites)
    vmem = pl.BlockSpec(memory_space=pltpu.VMEM)
    return pl.pallas_call(
        encode_kernel,
        out_shape=(
            jax.ShapeDtypeStruct((PAIRS, blocks, sites), jnp.int32),
            jax.ShapeDtypeStruct((number, 1, sites), jnp.float32),
        ),
        in_specs=[pl.BlockSpec(memory_space=pltpu.SMEM), vmem, vmem, vmem],
        out_specs=(vmem, pl.BlockSpec(memory_space=pl.ANY)),
        scratch_shapes=[
            pltpu.VMEM(share, jnp.float32),
            pltpu.VMEM((sites, sites), jnp.float32),
            pltpu.VMEM((number, 1, sites), jnp.float32),
            pltpu.SemaphoreType.DMA,
        ],
        compiler_params=pltpu.CompilerParams(vmem_limit_bytes=24 << 20),
        cost_estimate=pl.CostEstimate(
            flops=30 * SHARE * blocks * sites, bytes_accessed=14 * SHARE * blocks * sites, transcendentals=0
        ),
    )(member, forecasts, obs, weight)


def decode_kernel(member, sums_here, own, across, beside, corner, out, loss, sums, scores, held, arrived, left):
    come = [
        pltpu.make_async_copy(here, there, arrived.at[n])
        for n, (here, there) in enumerate(((sums_here, sums), (beside, held.at[0]), (corner, held.at[1])))
    ]
    for copy in come:
        copy.start()
    come[0].wait()
    halves = sums.shape[0] // MEMBERS
    totals = [sum(sums[m * halves + h] for h in range(halves)) for m in range(MEMBERS)]
    lane = lax.broadcasted_iota(jnp.int32, totals[0].shape, 1)

    def at(i):
        return jnp.sum(jnp.where(lane == i, totals[0], 0.0), keepdims=True)

    area = [at(SHARE + g) for g in range(2)]
    scale = [jnp.broadcast_to(at(SHARE + 2 + g) / area[g], own.shape[1:]) for g in range(2)]

    go = []
    for n, (partner, codes) in enumerate(((0, own), (2, across), (1, held.at[0]), (3, held.at[1]))):
        if n >= 2:
            come[n - 1].wait()
        first = (member[0] ^ partner) * SHARE
        unit = jnp.exp2((codes[PAIRS - 1] >> 16).astype(jnp.float32)) * (1.0 / TOP**4)
        units = [unit * scale[g] for g in range(2)]

        def write(i, code, n=n, first=first, units=units):
            steps = code.astype(jnp.float32)
            square = steps * steps
            unit = jnp.where(first + i >= ATMOS, units[1], units[0])
            scores[n, i] = (steps * jnp.abs(steps)) * square * unit

        def pair(i, carry, codes=codes, write=write):
            both = codes[i]
            write(i, (both << 16) >> 16)
            write(PAIRS + i, both >> 16)
            return carry

        lax.fori_loop(0, PAIRS - 1, pair, 0, unroll=True)
        write(PAIRS - 1, (codes[PAIRS - 1] << 16) >> 16)
        copy = pltpu.make_async_copy(scores.at[n], out.at[pl.ds(first, SHARE)], left.at[n])
        copy.start()
        go.append(copy)

    width = 3 * TILE_SITES
    channel = lax.broadcasted_iota(jnp.int32, (1, width), 1)
    wide = jnp.zeros((1, width), jnp.float32)
    blank = jnp.zeros((1, width - TILE_SITES), jnp.float32)
    for m in range(MEMBERS):
        moved = pltpu.roll(jnp.concatenate([totals[m], blank], axis=1), m * SHARE, 1)
        wide = jnp.where((channel >= m * SHARE) & (channel < (m + 1) * SHARE), moved, wide)
    wide = wide / jnp.where(channel >= ATMOS, area[1], area[0])
    loss[...] = wide[0, :VARIABLE_NUMBER]
    for copy in go:
        copy.wait()


def decode(member, sums, shares):
    blocks, sites = shares[0].shape[1:]
    vmem = pl.BlockSpec(memory_space=pltpu.VMEM)
    anywhere = pl.BlockSpec(memory_space=pl.ANY)
    return pl.pallas_call(
        decode_kernel,
        out_shape=(
            jax.ShapeDtypeStruct((VARIABLE_NUMBER, blocks, sites), jnp.float32),
            jax.ShapeDtypeStruct((VARIABLE_NUMBER,), jnp.float32),
        ),
        in_specs=[pl.BlockSpec(memory_space=pltpu.SMEM), anywhere, vmem, vmem, anywhere, anywhere],
        out_specs=(anywhere, vmem),
        scratch_shapes=[
            pltpu.VMEM(sums.shape, jnp.float32),
            pltpu.VMEM((MEMBERS, SHARE, blocks, sites), jnp.float32),
            pltpu.VMEM((2, *shares[0].shape), jnp.int32),
            pltpu.SemaphoreType.DMA((3,)),
            pltpu.SemaphoreType.DMA((MEMBERS,)),
        ],
        compiler_params=pltpu.CompilerParams(vmem_limit_bytes=24 << 20),
        cost_estimate=pl.CostEstimate(
            flops=64 * shares[0].size, bytes_accessed=48 * shares[0].size, transcendentals=0
        ),
    )(member, sums, *shares)


def copied(row, number):
    return jnp.broadcast_to(row[None], (number, *row.shape))


def exchanged(copies, axes):
    return lax.all_to_all(copies, axes, split_axis=0, concat_axis=0, tiled=True)


def in_one_step(always, f, *args):
    shapes = jax.eval_shape(f, *args)
    return lax.cond(always, f, lambda *args: jax.tree.map(lambda x: jnp.zeros(x.shape, x.dtype), shapes), *args)


def shards(ensemble_prediction, observed_analysis, validity_flags):
    blocks_here = observed_analysis.shape[1]
    forecasts = lax.all_to_all(ensemble_prediction[0], "member", split_axis=0, concat_axis=0, tiled=True)
    forecasts = forecasts.reshape(MEMBERS, SHARE, *forecasts.shape[1:])

    first_point = lax.axis_index(SPACE) * (blocks_here * TILE_SITES)
    position = first_point + jnp.arange(blocks_here * TILE_SITES, dtype=jnp.int32).reshape(
        blocks_here, TILE_SITES
    )
    inside = (position < ROWS * LON).astype(jnp.float32)
    lat_row = (position // LON).astype(jnp.float32)
    cosine = jnp.cos(jnp.pi * ((lat_row + 0.5) / ROWS - 0.5))
    weight = (cosine * inside)[None] * (validity_flags > 0).astype(jnp.float32)

    member = lax.axis_index("member")[None]
    codes, partial = encode(
        member, forecasts, observed_analysis, weight, REPEATS * lax.axis_size(ALONG_ZX)
    )
    always = member[0] >= 0
    across = lax.ppermute(codes, "member", ACROSS)

    def add_up_and_send(codes, copies):
        beside = lax.ppermute(codes, "member", BESIDE)
        corner = lax.ppermute(codes, "member", CORNER)
        over_zx = jnp.sum(exchanged(copies, ALONG_ZX)[::REPEATS], axis=0)
        over_zx = copied(over_zx, lax.axis_size(ALONG_YC))
        return beside, corner, in_one_step(always, lambda copies: exchanged(copies, ALONG_YC), over_zx)

    beside, corner, over_yc = in_one_step(always, add_up_and_send, codes, partial)
    point_score, loss = decode(member, over_yc, (codes, across, beside, corner))
    return (point_score, loss)


def solution(mesh):
    split = Mesh(
        mesh.devices.reshape(mesh.shape["member"], 8, 2, 4, 2),
        ("member", "space_0", "space_1", "space_2", "space_3"),
    )
    return jax.shard_map(
        shards,
        mesh=split,
        in_specs=(P("member", None, SPACE, None), P(None, SPACE, None), P(None, SPACE, None)),
        out_specs=(P(None, SPACE, None), P()),
        check_vma=False,
    )
```

```python
import jax
import jax.numpy as jnp
from jax import lax
from jax.experimental import pallas as pl
from jax.experimental.pallas import tpu as pltpu
from jax.sharding import Mesh
from jax.sharding import PartitionSpec as P

VARIABLE_NUMBER = 300
ATMOS = 180
TILE_SITES = 128
LON = 720
ROWS = 360
MEMBERS = 4
SHARE = VARIABLE_NUMBER // MEMBERS
SPACE = ("space_0", "space_1", "space_2", "space_3")
ALONG_ZX = ("space_0", "space_2")
ALONG_YC = ("member", "space_1", "space_3")
COEFF = (1.0 - 0.05 / MEMBERS) / (2.0 * MEMBERS * (MEMBERS - 1))
TOP = 32767.0
BESIDE = [(m, m ^ 1) for m in range(MEMBERS)]
ACROSS = [(m, m ^ 2) for m in range(MEMBERS)]
CORNER = [(m, m ^ 3) for m in range(MEMBERS)]
REPEATS = 10
LEAST_EXPONENT = -120.0
PAIRS = (SHARE + 1) // 2


def encode_kernel(member, forecasts, obs, weight, codes, partial, values, rows, held, copied):
    first = member[0] * SHARE

    def score(i, top):
        target = obs[first + i].astype(jnp.float32)
        a, b, c, d = (forecasts[m, i].astype(jnp.float32) for m in range(MEMBERS))
        skill = jnp.abs(a - target) + jnp.abs(b - target) + jnp.abs(c - target) + jnp.abs(d - target)
        low_ab, high_ab = jnp.minimum(a, b), jnp.maximum(a, b)
        low_cd, high_cd = jnp.minimum(c, d), jnp.maximum(c, d)
        outer = jnp.maximum(high_ab, high_cd) - jnp.minimum(low_ab, low_cd)
        inner = jnp.abs(jnp.minimum(high_ab, high_cd) - jnp.maximum(low_ab, low_cd))
        spread = 3.0 * outer + inner
        group = (first + i >= ATMOS).astype(jnp.int32)
        value = (skill * (1.0 / MEMBERS) - (2.0 * COEFF) * spread) * weight[group]
        values[i] = value
        rows[pl.ds(i, 1), :] = jnp.sum(value, axis=0, keepdims=True)
        return jnp.maximum(top, jnp.abs(value))

    rows[...] = jnp.zeros(rows.shape, jnp.float32)
    top = lax.fori_loop(0, SHARE, score, jnp.zeros(values.shape[1:], jnp.float32), unroll=5)
    for g in range(2):
        rows[SHARE + g : SHARE + g + 1, :] = jnp.sum(weight[g], axis=0, keepdims=True)
        valid = (weight[g] > 0.0).astype(jnp.float32)
        rows[SHARE + 2 + g : SHARE + 3 + g, :] = jnp.sum(valid, axis=0, keepdims=True)
    ones = jnp.ones((8, TILE_SITES), jnp.float32)
    sums = lax.dot_general(
        ones, rows[...], (((1,), (1,)), ((), ())), precision=lax.Precision.HIGHEST, preferred_element_type=jnp.float32
    )
    held[...] = jnp.broadcast_to(sums[None, :1], held.shape)
    copy = pltpu.make_async_copy(held, partial, copied)
    copy.start()

    top = jnp.broadcast_to(jnp.max(top, keepdims=True), top.shape)
    k = jnp.where(top > 0.0, jnp.ceil(jnp.log2(jnp.where(top > 0.0, top, 1.0))), 0.0)
    k = jnp.maximum(k, LEAST_EXPONENT)
    shrink = jnp.exp2(-k)

    def code(value):
        root = jnp.sqrt(jnp.sqrt(jnp.abs(value) * shrink))
        steps = jnp.minimum(root * TOP + 0.5, TOP)
        return jnp.where(value < 0.0, -steps, steps).astype(jnp.int32)

    def pair(i, carry):
        codes[i] = (code(values[PAIRS + i]) << 16) | (code(values[i]) & 0xFFFF)
        return carry

    lax.fori_loop(0, PAIRS - 1, pair, 0, unroll=4)
    codes[PAIRS - 1] = (k.astype(jnp.int32) << 16) | (code(values[PAIRS - 1]) & 0xFFFF)
    copy.wait()


def encode(member, forecasts, obs, weight, number):
    blocks, sites = obs.shape[1:]
    share = (SHARE, blocks, sites)
    vmem = pl.BlockSpec(memory_space=pltpu.VMEM)
    return pl.pallas_call(
        encode_kernel,
        out_shape=(
            jax.ShapeDtypeStruct((PAIRS, blocks, sites), jnp.int32),
            jax.ShapeDtypeStruct((number, 1, sites), jnp.float32),
        ),
        in_specs=[pl.BlockSpec(memory_space=pltpu.SMEM), vmem, vmem, vmem],
        out_specs=(vmem, pl.BlockSpec(memory_space=pl.ANY)),
        scratch_shapes=[
            pltpu.VMEM(share, jnp.float32),
            pltpu.VMEM((sites, sites), jnp.float32),
            pltpu.VMEM((number, 1, sites), jnp.float32),
            pltpu.SemaphoreType.DMA,
        ],
        compiler_params=pltpu.CompilerParams(vmem_limit_bytes=24 << 20),
        cost_estimate=pl.CostEstimate(
            flops=30 * SHARE * blocks * sites, bytes_accessed=14 * SHARE * blocks * sites, transcendentals=0
        ),
    )(member, forecasts, obs, weight)


def decode_kernel(member, sums_here, own, across, beside, corner, out, loss, sums, scores, held, arrived, left):
    come = [
        pltpu.make_async_copy(here, there, arrived.at[n])
        for n, (here, there) in enumerate(((sums_here, sums), (beside, held.at[0]), (corner, held.at[1])))
    ]
    for copy in come:
        copy.start()
    come[0].wait()
    halves = sums.shape[0] // MEMBERS
    totals = [sum(sums[m * halves + h] for h in range(halves)) for m in range(MEMBERS)]
    lane = lax.broadcasted_iota(jnp.int32, totals[0].shape, 1)

    def at(i):
        return jnp.sum(jnp.where(lane == i, totals[0], 0.0), keepdims=True)

    area = [at(SHARE + g) for g in range(2)]
    scale = [jnp.broadcast_to(at(SHARE + 2 + g) / area[g], own.shape[1:]) for g in range(2)]

    go = []
    for n, (partner, codes) in enumerate(((0, own), (2, across), (1, held.at[0]), (3, held.at[1]))):
        if n >= 2:
            come[n - 1].wait()
        first = (member[0] ^ partner) * SHARE
        unit = jnp.exp2((codes[PAIRS - 1] >> 16).astype(jnp.float32)) * (1.0 / TOP**4)
        units = [unit * scale[g] for g in range(2)]

        def write(i, code, n=n, first=first, units=units):
            steps = code.astype(jnp.float32)
            square = steps * steps
            unit = jnp.where(first + i >= ATMOS, units[1], units[0])
            scores[n, i] = (steps * jnp.abs(steps)) * square * unit

        def pair(i, carry, codes=codes, write=write):
            both = codes[i]
            write(i, (both << 16) >> 16)
            write(PAIRS + i, both >> 16)
            return carry

        lax.fori_loop(0, PAIRS - 1, pair, 0, unroll=True)
        write(PAIRS - 1, (codes[PAIRS - 1] << 16) >> 16)
        copy = pltpu.make_async_copy(scores.at[n], out.at[pl.ds(first, SHARE)], left.at[n])
        copy.start()
        go.append(copy)

    width = 3 * TILE_SITES
    channel = lax.broadcasted_iota(jnp.int32, (1, width), 1)
    wide = jnp.zeros((1, width), jnp.float32)
    blank = jnp.zeros((1, width - TILE_SITES), jnp.float32)
    for m in range(MEMBERS):
        moved = pltpu.roll(jnp.concatenate([totals[m], blank], axis=1), m * SHARE, 1)
        wide = jnp.where((channel >= m * SHARE) & (channel < (m + 1) * SHARE), moved, wide)
    wide = wide / jnp.where(channel >= ATMOS, area[1], area[0])
    loss[...] = wide[0, :VARIABLE_NUMBER]
    for copy in go:
        copy.wait()


def decode(member, sums, shares):
    blocks, sites = shares[0].shape[1:]
    vmem = pl.BlockSpec(memory_space=pltpu.VMEM)
    anywhere = pl.BlockSpec(memory_space=pl.ANY)
    return pl.pallas_call(
        decode_kernel,
        out_shape=(
            jax.ShapeDtypeStruct((VARIABLE_NUMBER, blocks, sites), jnp.float32),
            jax.ShapeDtypeStruct((VARIABLE_NUMBER,), jnp.float32),
        ),
        in_specs=[pl.BlockSpec(memory_space=pltpu.SMEM), anywhere, vmem, vmem, anywhere, anywhere],
        out_specs=(anywhere, vmem),
        scratch_shapes=[
            pltpu.VMEM(sums.shape, jnp.float32),
            pltpu.VMEM((MEMBERS, SHARE, blocks, sites), jnp.float32),
            pltpu.VMEM((2, *shares[0].shape), jnp.int32),
            pltpu.SemaphoreType.DMA((3,)),
            pltpu.SemaphoreType.DMA((MEMBERS,)),
        ],
        compiler_params=pltpu.CompilerParams(vmem_limit_bytes=24 << 20),
        cost_estimate=pl.CostEstimate(
            flops=64 * shares[0].size, bytes_accessed=48 * shares[0].size, transcendentals=0
        ),
    )(member, sums, *shares)


def copied(row, number):
    return jnp.broadcast_to(row[None], (number, *row.shape))


def exchanged(copies, axes):
    return lax.all_to_all(copies, axes, split_axis=0, concat_axis=0, tiled=True)


def in_one_step(always, f, *args):
    shapes = jax.eval_shape(f, *args)
    return lax.cond(always, f, lambda *args: jax.tree.map(lambda x: jnp.zeros(x.shape, x.dtype), shapes), *args)


def shards(ensemble_prediction, observed_analysis, validity_flags):
    blocks_here = observed_analysis.shape[1]
    forecasts = lax.all_to_all(ensemble_prediction[0], "member", split_axis=0, concat_axis=0, tiled=True)
    forecasts = forecasts.reshape(MEMBERS, SHARE, *forecasts.shape[1:])

    first_point = lax.axis_index(SPACE) * (blocks_here * TILE_SITES)
    position = first_point + jnp.arange(blocks_here * TILE_SITES, dtype=jnp.int32).reshape(
        blocks_here, TILE_SITES
    )
    inside = (position < ROWS * LON).astype(jnp.float32)
    lat_row = (position // LON).astype(jnp.float32)
    cosine = jnp.cos(jnp.pi * ((lat_row + 0.5) / ROWS - 0.5))
    weight = (cosine * inside)[None] * (validity_flags > 0).astype(jnp.float32)

    member = lax.axis_index("member")[None]
    codes, partial = encode(
        member, forecasts, observed_analysis, weight, REPEATS * lax.axis_size(ALONG_ZX)
    )
    always = member[0] >= 0
    across = lax.ppermute(codes, "member", ACROSS)

    def add_up_and_send(codes, copies):
        beside = lax.ppermute(codes, "member", BESIDE)
        corner = lax.ppermute(codes, "member", CORNER)
        over_zx = jnp.sum(exchanged(copies, ALONG_ZX)[::REPEATS], axis=0)
        over_zx = copied(over_zx, lax.axis_size(ALONG_YC))
        return beside, corner, in_one_step(always, lambda copies: exchanged(copies, ALONG_YC), over_zx)

    beside, corner, over_yc = in_one_step(always, add_up_and_send, codes, partial)
    point_score, loss = decode(member, over_yc, (codes, across, beside, corner))
    return (point_score, loss)


def solution(mesh):
    split = Mesh(
        mesh.devices.reshape(mesh.shape["member"], 8, 2, 4, 2),
        ("member", "space_0", "space_1", "space_2", "space_3"),
    )
    return jax.shard_map(
        shards,
        mesh=split,
        in_specs=(P("member", None, SPACE, None), P(None, SPACE, None), P(None, SPACE, None)),
        out_specs=(P(None, SPACE, None), P()),
        check_vma=False,
    )
```

```python
import jax
import jax.numpy as jnp
from jax import lax
from jax.experimental import pallas as pl
from jax.experimental.pallas import tpu as pltpu
from jax.sharding import Mesh
from jax.sharding import PartitionSpec as P

VARIABLE_NUMBER = 300
ATMOS = 180
TILE_SITES = 128
LON = 720
ROWS = 360
MEMBERS = 4
SHARE = VARIABLE_NUMBER // MEMBERS
SPACE = ("space_0", "space_1", "space_2", "space_3")
ALONG_ZX = ("space_0", "space_2")
ALONG_YC = ("member", "space_1", "space_3")
COEFF = (1.0 - 0.05 / MEMBERS) / (2.0 * MEMBERS * (MEMBERS - 1))
TOP = 32767.0
BESIDE = [(m, m ^ 1) for m in range(MEMBERS)]
ACROSS = [(m, m ^ 2) for m in range(MEMBERS)]
CORNER = [(m, m ^ 3) for m in range(MEMBERS)]
REPEATS = 10
LEAST_EXPONENT = -120.0
PAIRS = (SHARE + 1) // 2


def encode_kernel(member, forecasts, obs, weight, codes, partial, values, rows, held, copied):
    first = member[0] * SHARE

    def score(i, top):
        target = obs[first + i].astype(jnp.float32)
        a, b, c, d = (forecasts[m, i].astype(jnp.float32) for m in range(MEMBERS))
        skill = jnp.abs(a - target) + jnp.abs(b - target) + jnp.abs(c - target) + jnp.abs(d - target)
        low_ab, high_ab = jnp.minimum(a, b), jnp.maximum(a, b)
        low_cd, high_cd = jnp.minimum(c, d), jnp.maximum(c, d)
        outer = jnp.maximum(high_ab, high_cd) - jnp.minimum(low_ab, low_cd)
        inner = jnp.abs(jnp.minimum(high_ab, high_cd) - jnp.maximum(low_ab, low_cd))
        spread = 3.0 * outer + inner
        group = (first + i >= ATMOS).astype(jnp.int32)
        value = (skill * (1.0 / MEMBERS) - (2.0 * COEFF) * spread) * weight[group]
        values[i] = value
        rows[pl.ds(i, 1), :] = jnp.sum(value, axis=0, keepdims=True)
        return jnp.maximum(top, jnp.abs(value))

    rows[...] = jnp.zeros(rows.shape, jnp.float32)
    top = lax.fori_loop(0, SHARE, score, jnp.zeros(values.shape[1:], jnp.float32), unroll=3)
    for g in range(2):
        rows[SHARE + g : SHARE + g + 1, :] = jnp.sum(weight[g], axis=0, keepdims=True)
        valid = (weight[g] > 0.0).astype(jnp.float32)
        rows[SHARE + 2 + g : SHARE + 3 + g, :] = jnp.sum(valid, axis=0, keepdims=True)
    ones = jnp.ones((8, TILE_SITES), jnp.float32)
    sums = lax.dot_general(
        ones, rows[...], (((1,), (1,)), ((), ())), precision=lax.Precision.HIGHEST, preferred_element_type=jnp.float32
    )
    held[...] = jnp.broadcast_to(sums[None, :1], held.shape)
    copy = pltpu.make_async_copy(held, partial, copied)
    copy.start()

    top = jnp.broadcast_to(jnp.max(top, keepdims=True), top.shape)
    k = jnp.where(top > 0.0, jnp.ceil(jnp.log2(jnp.where(top > 0.0, top, 1.0))), 0.0)
    k = jnp.maximum(k, LEAST_EXPONENT)
    shrink = jnp.exp2(-k)

    def code(value):
        root = jnp.sqrt(jnp.sqrt(jnp.abs(value) * shrink))
        steps = jnp.minimum(root * TOP + 0.5, TOP)
        return jnp.where(value < 0.0, -steps, steps).astype(jnp.int32)

    def pair(i, carry):
        codes[i] = (code(values[PAIRS + i]) << 16) | (code(values[i]) & 0xFFFF)
        return carry

    lax.fori_loop(0, PAIRS - 1, pair, 0, unroll=4)
    codes[PAIRS - 1] = (k.astype(jnp.int32) << 16) | (code(values[PAIRS - 1]) & 0xFFFF)
    copy.wait()


def encode(member, forecasts, obs, weight, number):
    blocks, sites = obs.shape[1:]
    share = (SHARE, blocks, sites)
    vmem = pl.BlockSpec(memory_space=pltpu.VMEM)
    return pl.pallas_call(
        encode_kernel,
        out_shape=(
            jax.ShapeDtypeStruct((PAIRS, blocks, sites), jnp.int32),
            jax.ShapeDtypeStruct((number, 1, sites), jnp.float32),
        ),
        in_specs=[pl.BlockSpec(memory_space=pltpu.SMEM), vmem, vmem, vmem],
        out_specs=(vmem, pl.BlockSpec(memory_space=pl.ANY)),
        scratch_shapes=[
            pltpu.VMEM(share, jnp.float32),
            pltpu.VMEM((sites, sites), jnp.float32),
            pltpu.VMEM((number, 1, sites), jnp.float32),
            pltpu.SemaphoreType.DMA,
        ],
        compiler_params=pltpu.CompilerParams(vmem_limit_bytes=24 << 20),
        cost_estimate=pl.CostEstimate(
            flops=30 * SHARE * blocks * sites, bytes_accessed=14 * SHARE * blocks * sites, transcendentals=0
        ),
    )(member, forecasts, obs, weight)


def decode_kernel(member, sums_here, own, across, beside, corner, out, loss, sums, scores, held, arrived, left):
    come = [
        pltpu.make_async_copy(here, there, arrived.at[n])
        for n, (here, there) in enumerate(((sums_here, sums), (beside, held.at[0]), (corner, held.at[1])))
    ]
    for copy in come:
        copy.start()
    come[0].wait()
    halves = sums.shape[0] // MEMBERS
    totals = [sum(sums[m * halves + h] for h in range(halves)) for m in range(MEMBERS)]
    lane = lax.broadcasted_iota(jnp.int32, totals[0].shape, 1)

    def at(i):
        return jnp.sum(jnp.where(lane == i, totals[0], 0.0), keepdims=True)

    area = [at(SHARE + g) for g in range(2)]
    scale = [jnp.broadcast_to(at(SHARE + 2 + g) / area[g], own.shape[1:]) for g in range(2)]

    go = []
    for n, (partner, codes) in enumerate(((0, own), (2, across), (1, held.at[0]), (3, held.at[1]))):
        if n >= 2:
            come[n - 1].wait()
        first = (member[0] ^ partner) * SHARE
        unit = jnp.exp2((codes[PAIRS - 1] >> 16).astype(jnp.float32)) * (1.0 / TOP**4)
        units = [unit * scale[g] for g in range(2)]

        def write(i, code, n=n, first=first, units=units):
            steps = code.astype(jnp.float32)
            square = steps * steps
            unit = jnp.where(first + i >= ATMOS, units[1], units[0])
            scores[n, i] = (steps * jnp.abs(steps)) * square * unit

        def pair(i, carry, codes=codes, write=write):
            both = codes[i]
            write(i, (both << 16) >> 16)
            write(PAIRS + i, both >> 16)
            return carry

        lax.fori_loop(0, PAIRS - 1, pair, 0, unroll=True)
        write(PAIRS - 1, (codes[PAIRS - 1] << 16) >> 16)
        copy = pltpu.make_async_copy(scores.at[n], out.at[pl.ds(first, SHARE)], left.at[n])
        copy.start()
        go.append(copy)

    width = 3 * TILE_SITES
    channel = lax.broadcasted_iota(jnp.int32, (1, width), 1)
    wide = jnp.zeros((1, width), jnp.float32)
    blank = jnp.zeros((1, width - TILE_SITES), jnp.float32)
    for m in range(MEMBERS):
        moved = pltpu.roll(jnp.concatenate([totals[m], blank], axis=1), m * SHARE, 1)
        wide = jnp.where((channel >= m * SHARE) & (channel < (m + 1) * SHARE), moved, wide)
    wide = wide / jnp.where(channel >= ATMOS, area[1], area[0])
    loss[...] = wide[0, :VARIABLE_NUMBER]
    for copy in go:
        copy.wait()


def decode(member, sums, shares):
    blocks, sites = shares[0].shape[1:]
    vmem = pl.BlockSpec(memory_space=pltpu.VMEM)
    anywhere = pl.BlockSpec(memory_space=pl.ANY)
    return pl.pallas_call(
        decode_kernel,
        out_shape=(
            jax.ShapeDtypeStruct((VARIABLE_NUMBER, blocks, sites), jnp.float32),
            jax.ShapeDtypeStruct((VARIABLE_NUMBER,), jnp.float32),
        ),
        in_specs=[pl.BlockSpec(memory_space=pltpu.SMEM), anywhere, vmem, vmem, anywhere, anywhere],
        out_specs=(anywhere, vmem),
        scratch_shapes=[
            pltpu.VMEM(sums.shape, jnp.float32),
            pltpu.VMEM((MEMBERS, SHARE, blocks, sites), jnp.float32),
            pltpu.VMEM((2, *shares[0].shape), jnp.int32),
            pltpu.SemaphoreType.DMA((3,)),
            pltpu.SemaphoreType.DMA((MEMBERS,)),
        ],
        compiler_params=pltpu.CompilerParams(vmem_limit_bytes=24 << 20),
        cost_estimate=pl.CostEstimate(
            flops=64 * shares[0].size, bytes_accessed=48 * shares[0].size, transcendentals=0
        ),
    )(member, sums, *shares)


def copied(row, number):
    return jnp.broadcast_to(row[None], (number, *row.shape))


def exchanged(copies, axes):
    return lax.all_to_all(copies, axes, split_axis=0, concat_axis=0, tiled=True)


def in_one_step(always, f, *args):
    shapes = jax.eval_shape(f, *args)
    return lax.cond(always, f, lambda *args: jax.tree.map(lambda x: jnp.zeros(x.shape, x.dtype), shapes), *args)


def shards(ensemble_prediction, observed_analysis, validity_flags):
    blocks_here = observed_analysis.shape[1]
    forecasts = lax.all_to_all(ensemble_prediction[0], "member", split_axis=0, concat_axis=0, tiled=True)
    forecasts = forecasts.reshape(MEMBERS, SHARE, *forecasts.shape[1:])

    first_point = lax.axis_index(SPACE) * (blocks_here * TILE_SITES)
    position = first_point + jnp.arange(blocks_here * TILE_SITES, dtype=jnp.int32).reshape(
        blocks_here, TILE_SITES
    )
    inside = (position < ROWS * LON).astype(jnp.float32)
    lat_row = (position // LON).astype(jnp.float32)
    cosine = jnp.cos(jnp.pi * ((lat_row + 0.5) / ROWS - 0.5))
    weight = (cosine * inside)[None] * (validity_flags > 0).astype(jnp.float32)

    member = lax.axis_index("member")[None]
    codes, partial = encode(
        member, forecasts, observed_analysis, weight, REPEATS * lax.axis_size(ALONG_ZX)
    )
    always = member[0] >= 0
    across = lax.ppermute(codes, "member", ACROSS)

    def add_up_and_send(codes, copies):
        beside = lax.ppermute(codes, "member", BESIDE)
        corner = lax.ppermute(codes, "member", CORNER)
        over_zx = jnp.sum(exchanged(copies, ALONG_ZX)[::REPEATS], axis=0)
        over_zx = copied(over_zx, lax.axis_size(ALONG_YC))
        return beside, corner, in_one_step(always, lambda copies: exchanged(copies, ALONG_YC), over_zx)

    beside, corner, over_yc = in_one_step(always, add_up_and_send, codes, partial)
    point_score, loss = decode(member, over_yc, (codes, across, beside, corner))
    return (point_score, loss)


def solution(mesh):
    split = Mesh(
        mesh.devices.reshape(mesh.shape["member"], 8, 2, 4, 2),
        ("member", "space_0", "space_1", "space_2", "space_3"),
    )
    return jax.shard_map(
        shards,
        mesh=split,
        in_specs=(P("member", None, SPACE, None), P(None, SPACE, None), P(None, SPACE, None)),
        out_specs=(P(None, SPACE, None), P()),
        check_vma=False,
    )
```
